128 devices in a mesh: dom: 8 (over y, core), order: 16 (over z, x).
Axes of the slice: x: 4, y: 4, z: 4, core: 2. Of those that a mesh axis runs over, the one named last changes fastest.
Arguments:
- ssh: float32 [8192, 16, 256], P(('dom', 'order')), may hold values from -6 to 6
- cell_count: int32 [8192], P(('dom', 'order')), may hold values from 1 to 256, 1572864 in all
- remap_index: int32 [8192, 4, 256], P(('dom', 'order')), may hold values from 0 to 255
- remap_weight: float32 [8192, 4, 256], P(('dom', 'order')), may hold values from 0.1 to 0.6
- block_tile: int32 [8192], P(('dom', 'order')), may hold values from 0 to 32767, as said below
- gauss_weight: float32 [1024], replicated, may hold values from 0.2 to 2
- love: float32 [1024], replicated, may hold values from 0.3 to 3
- legendre: bfloat16 [1024, 1024, 1024], P(('dom', 'order')), may hold values from -0.1875 to 0.1875
Outputs:
- sal: float32 [8192, 16, 256], P(('dom', 'order'))
The draws below stay inside these ranges and needn't reach their ends.
Inputs may be any that keep to these rules, and one draw needn't show every extreme that they name: Block rows p * 64 to (p + 1) * 64 - 1 name tiles whose owner block_tile // 256 is p - 1, p or p + 1; exactly 32 of them name owner p, and at most 32 name each of the other two.
All inputs are finite; a program needn't handle non-finite values. No bound on the sum of `cell_count` on one device may be relied on, other than what follows from the above.
Results may differ from the reference program's by a relative error of at most 0.006.
Values may be sent and summed in bfloat16 or wider, within the bound.
No kernel may reach another device: no remote copies, remote signals or barrier semaphores. Data moves between devices by JAX's collectives and lax.ppermute only.
A program may use at most 192 MiB of HBM per device.

```python
import math
import jax
import jax.numpy as jnp
import numpy as np
from jax import lax

NLON = 4096
ORDERS = 1024
DEGREES = 1024
BLOCK = 256
KPTS = 4
NF = 16
BLK_DEV = 64
CAP = 32
TILE_DEV = 256
BLOCKS = 8192
LATS = 2048
HALF = 1024
N_DOM = 8
N_ORDER = 16


def draw_block_tile(key, part):
    device_count = N_DOM * N_ORDER
    key_lower = jax.random.fold_in(key, 11)
    key_shuffle = jax.random.fold_in(key, 12)
    key_local = jax.random.fold_in(key, 13)
    lower_count = jax.random.randint(key_lower, (device_count,), 0, CAP + 1)
    device = jnp.arange(device_count, dtype=jnp.int32)
    lower_count = jnp.where(device == 0, 0, jnp.where(device == device_count - 1, CAP, lower_count))
    slot_idx = jnp.arange(BLK_DEV, dtype=jnp.int32)[None, :]
    offset = jnp.where(slot_idx < CAP, 0, jnp.where(slot_idx < CAP + lower_count[:, None], -1, 1))
    perm_keys = jax.random.split(key_shuffle, device_count)
    shuffle = jax.vmap(lambda one_key: jax.random.permutation(one_key, BLK_DEV))(perm_keys)
    offset = jnp.take_along_axis(offset, shuffle.astype(jnp.int32), axis=1)
    owner_rank = device[:, None] + offset
    local_tile = jax.random.randint(key_local, (device_count, BLK_DEV), 0, TILE_DEV)
    return (owner_rank * TILE_DEV + local_tile).reshape(-1).astype(jnp.int32)


def touch_ends(array, key, smallest, high):
    place = [jax.random.randint(jax.random.fold_in(key, axis), (), 0, length) for axis, length in enumerate(array.shape)]
    main_axis = array.shape.index(max(array.shape))
    beside = place[:main_axis] + [(place[main_axis] + 1) % array.shape[main_axis]] + place[main_axis + 1:]
    return array.at[tuple(place)].set(smallest).at[tuple(beside)].set(high)


def shard_levels(own_key, extent, cuts, least, high):
    gain, own = 1.0, jax.random.fold_in(own_key, 6)
    for dim, parts in cuts:
        steps = jnp.exp(jax.random.uniform(jax.random.fold_in(own, dim), (parts,), jnp.float32, least / len(cuts), high / len(cuts)))
        gain = gain * jnp.repeat(steps, extent[dim] // parts).reshape([-1 if axis == dim else 1 for axis in range(len(extent))])
    return gain


def length_profile(amount, total, limit, lean):
    portions = [(1 << 20) // math.isqrt(standing ** lean) + 1 for standing in range(2, amount + 1)]
    surplus, given = total - limit - (amount - 1), [1] * (amount - 1)
    while surplus > 0:
        free = [i for i in range(amount - 1) if given[i] < limit]
        whole, budget = sum([portions[i] for i in free]), surplus
        for i in free:
            more = min(limit - given[i], max(1, budget * portions[i] // whole), surplus)
            given[i] = given[i] + more
            surplus = surplus - more
    return np.array([limit] + given)


def uneven(key, amount, total, most, skew):
    if amount == 2:
        one = jax.random.randint(key, (), max(1, total - most), min(most, total - 1) + 1)
        return jnp.stack([one, total - one])
    lengths = jnp.asarray(length_profile(amount, total, most, skew), jnp.int32)
    couples = (amount - 1) // 2
    source_of, taker = lengths[1:1 + 2 * couples:2], lengths[2:2 + 2 * couples:2]
    room = jnp.minimum(source_of - 1, most - taker)
    moved = jax.random.randint(jax.random.fold_in(key, 1), (couples,), 0, 1 << 20) % (room + 1)
    lengths = lengths.at[1:1 + 2 * couples:2].set(source_of - moved).at[2:2 + 2 * couples:2].set(taker + moved)
    return lengths[jax.random.permutation(jax.random.fold_in(key, 2), amount)]


def noise(own_key, dims, scale, limit, cuts=(), kind=jnp.bfloat16):
    gain = shard_levels(own_key, dims, cuts, -0.22, 0.18) if cuts else 1.0
    drawn = jax.random.normal(own_key, dims, jnp.float32) * scale * gain
    return jnp.minimum(jnp.maximum(drawn, -limit), limit).astype(kind)


def setup_inputs(seed: int = 0) -> dict:
    seeds = jax.random.split(jax.random.key(seed), 9)
    ssh = noise(seeds[0], (BLOCKS, NF, BLOCK), 1.0, 6.0, ((0, 128),), jnp.float32)
    cell_count = uneven(seeds[1], BLOCKS, BLOCKS * BLOCK * 3 // 4, BLOCK, 0).astype(jnp.int32)
    remap_index = touch_ends(jax.random.randint(seeds[2], (BLOCKS, KPTS, BLOCK), 0, BLOCK), jax.random.fold_in(seeds[2], 1), 0, BLOCK - 1).astype(jnp.int32)
    remap_weight = jnp.clip(0.1 + 0.5 * jax.random.uniform(seeds[3], (BLOCKS, KPTS, BLOCK), jnp.float32) ** shard_levels(seeds[3], (BLOCKS, KPTS, BLOCK), ((0, 128),), -0.2, 0.2), 0.1, 0.6)
    block_tile = draw_block_tile(jax.random.fold_in(seeds[8], 71), 0)
    gauss_weight = jnp.clip(jnp.exp(jax.random.uniform(seeds[5], (HALF,), jnp.float32, math.log(0.2), math.log(2.0))), 0.2, 2.0)
    love = jnp.clip(jnp.exp(jax.random.uniform(seeds[6], (DEGREES,), jnp.float32, math.log(0.3), math.log(3.0))), 0.3, 3.0)
    legendre = noise(seeds[7], (ORDERS, HALF, DEGREES), HALF ** -0.5, 0.1875, ((0, 128),))
    return dict(ssh=ssh, cell_count=cell_count, remap_index=remap_index, remap_weight=remap_weight, block_tile=block_tile, gauss_weight=gauss_weight, love=love, legendre=legendre)


def cell_matrix(remap_index, remap_weight, cell_count):
    block_count, point_count, num_cells = remap_index.shape
    points = lax.broadcasted_iota(jnp.int32, (1, 1, num_cells), 2)
    cell_idx = lax.broadcasted_iota(jnp.int32, (block_count, num_cells), 1)
    live_mask = (cell_idx < cell_count[:, None]).astype(jnp.float32)
    matrix = jnp.zeros((block_count, num_cells, num_cells), jnp.float32)
    for kpoint in range(point_count):
        hit_mask = remap_index[:, kpoint, :, None] == points
        matrix = matrix + jnp.where(hit_mask, remap_weight[:, kpoint, :, None], jnp.float32(0.0))
    return matrix * live_mask[:, :, None]


def fourier_tables(circle_len, order_count, tile_len):
    spots = lax.broadcasted_iota(jnp.int32, (circle_len, order_count), 0)
    waves = lax.broadcasted_iota(jnp.int32, (circle_len, order_count), 1)
    phase_idx = (spots * waves) % circle_len
    angles = phase_idx.astype(jnp.float32) * jnp.float32(2.0 * math.pi / circle_len)
    cosine = jnp.cos(angles)
    sine_part = jnp.sin(angles)
    forward = jnp.stack([cosine, -sine_part], axis=1) / jnp.float32(circle_len)
    forward = forward.reshape(circle_len // tile_len, tile_len, 2, order_count)
    factor = jnp.where(waves == 0, jnp.float32(1.0), jnp.float32(2.0))
    inverse = jnp.stack([cosine * factor, -sine_part * factor], axis=0)
    inverse = inverse.reshape(2, circle_len // tile_len, tile_len, order_count)
    return forward, inverse


def split_table(table):
    upper_part = table.astype(jnp.bfloat16)
    lower_part = (table - upper_part.astype(jnp.float32)).astype(jnp.bfloat16)
    return upper_part, lower_part


def legendre_order(tables, lat_rows, gauss_weight, love, first_order):
    half_lats = tables.shape[0]
    north_rows = lat_rows[:half_lats].astype(jnp.float32)
    south_rows = jnp.flip(lat_rows[half_lats:], axis=0).astype(jnp.float32)
    weights_col = gauss_weight[:, None]
    even_in = ((north_rows + south_rows) * weights_col).astype(jnp.bfloat16)
    odd_in = ((north_rows - south_rows) * weights_col).astype(jnp.bfloat16)
    table_wide = tables.astype(jnp.float32)
    even_coef = jnp.einsum('jl,jc->lc', table_wide, even_in.astype(jnp.float32))
    odd_coef = jnp.einsum('jl,jc->lc', table_wide, odd_in.astype(jnp.float32))
    degree = lax.broadcasted_iota(jnp.int32, (tables.shape[1], 1), 0)
    is_even = ((degree + first_order) % 2) == 0
    coefficient = jnp.where(degree < first_order, jnp.float32(0.0), jnp.where(is_even, even_coef, odd_coef))
    coefficient = (coefficient * love[:, None]).astype(jnp.bfloat16)
    even_part = jnp.where(is_even, coefficient, jnp.zeros_like(coefficient)).astype(jnp.float32)
    odd_part = jnp.where(is_even, jnp.zeros_like(coefficient), coefficient).astype(jnp.float32)
    even_out = jnp.einsum('jl,lc->jc', table_wide, even_part)
    odd_out = jnp.einsum('jl,lc->jc', table_wide, odd_part)
    upper_rows = even_out + odd_out
    lower_rows = jnp.flip(even_out - odd_out, axis=0)
    return jnp.concatenate([upper_rows, lower_rows], axis=0).astype(jnp.bfloat16)


def reference(ssh, cell_count, remap_index, remap_weight, block_tile, gauss_weight, love, legendre):
    device_count = N_DOM * N_ORDER
    highest = lax.Precision.HIGHEST

    def grouped(values):
        return values.reshape((device_count, BLK_DEV) + values.shape[1:])

    def spread_group(inputs):
        heights, counts, indices, weights = inputs
        return jnp.einsum('bfc,bcp->bfp', heights, cell_matrix(indices, weights, counts), precision=highest)

    spread = lax.map(spread_group, (grouped(ssh), grouped(cell_count), grouped(remap_index), grouped(remap_weight)))
    spread = spread.reshape(BLOCKS, NF, BLOCK)
    grid_tiles = jax.ops.segment_sum(spread, block_tile, num_segments=TILE_DEV * device_count)
    grid_vals = grid_tiles.reshape(LATS, NLON // BLOCK, NF, BLOCK)
    forward, inverse = fourier_tables(NLON, ORDERS, BLOCK)
    fourier = jnp.einsum('rsfb,sbcm->rfcm', grid_vals, forward, precision=lax.Precision.HIGH).astype(jnp.bfloat16)
    by_order = fourier.transpose(3, 0, 1, 2).reshape(ORDERS, LATS, NF * 2)

    def one_order(inputs):
        tables, lat_rows, first_order = inputs
        return legendre_order(tables, lat_rows, gauss_weight, love, first_order)

    order_ids = jnp.arange(ORDERS, dtype=jnp.int32)
    synth = lax.map(one_order, (legendre, by_order, order_ids))
    returned = synth.reshape(ORDERS, LATS, NF, 2).transpose(1, 2, 3, 0).astype(jnp.float32)
    inv_upper, inv_lower = split_table(inverse)
    load_grid = jnp.einsum('rfcm,csbm->rsfb', returned, inv_upper.astype(jnp.float32), precision=highest)
    load_grid = load_grid + jnp.einsum('rfcm,csbm->rsfb', returned, inv_lower.astype(jnp.float32), precision=highest)
    load_tiles = load_grid.reshape(TILE_DEV * device_count, NF, BLOCK)
    block_vals = load_tiles[block_tile]

    def gather_group(inputs):
        values, counts, indices, weights = inputs
        return jnp.einsum('bcp,bfp->bfc', cell_matrix(indices, weights, counts), values, precision=highest)

    sal = lax.map(gather_group, (grouped(block_vals), grouped(cell_count), grouped(remap_index), grouped(remap_weight)))
    return sal.reshape(BLOCKS, NF, BLOCK)
```

```python
import functools
import math

import jax
import jax.numpy as jnp
import numpy as np
from jax import lax
from jax.experimental import pallas as pl
from jax.experimental.pallas import tpu as pltpu
from jax.sharding import PartitionSpec as P

AXES = ("dom", "order")
DEVS = 128
NF = 16
BLOCK = 256
BLK = 64
HALF_BLK = 32
TILES = 256
LAT = 16
ORD = 8
NLAT = 1024
NDEG = 1024
RADIX = 16
NQ = 64
STEP = 8
F32 = jnp.float32
BF16 = jnp.bfloat16
MIB = 1 << 20

SMEM = pltpu.SMEM
VMEM = pltpu.VMEM


def hi_lo(table):
    table = np.asarray(table, np.float32)
    hi = table.astype(jnp.bfloat16)
    lo = (table - hi.astype(np.float32)).astype(jnp.bfloat16)
    return hi, lo


def make_tables():
    tiles = np.arange(RADIX)
    comps = []
    for u in range(9):
        comps.append(np.cos(2 * np.pi * ((u * tiles) % RADIX) / RADIX))
    for u in range(1, 8):
        comps.append(-np.sin(2 * np.pi * ((u * tiles) % RADIX) / RADIX))
    first = np.kron(np.stack(comps), np.eye(NF))
    f_hi, f_lo = hi_lo(first / 4096.0)
    i_hi, i_lo = hi_lo(2.0 * first.T)
    points = np.arange(BLOCK)
    angle = 2 * np.pi * ((np.arange(NQ)[:, None] * points[None, :]) % BLOCK) / BLOCK
    cos, sin = np.cos(angle), np.sin(angle)
    second = np.concatenate(
        [np.concatenate([cos, sin], axis=1), np.concatenate([-sin, cos], axis=1)], axis=0
    )
    s_hi, s_lo = hi_lo(second)
    twist = 2 * np.pi * (tiles[:, None] * points[None, :]) / 4096.0
    return dict(
        first=np.concatenate([f_hi, f_lo], axis=0),
        last=np.concatenate([i_hi, i_lo], axis=1),
        second=np.concatenate([s_hi, s_lo], axis=0),
        twc=np.cos(twist).astype(np.float32),
        tws=np.sin(twist).astype(np.float32),
    )


def vmem_spec():
    return pl.BlockSpec(memory_space=VMEM)


def smem_spec():
    return pl.BlockSpec(memory_space=SMEM)


def params(mib):
    return pltpu.CompilerParams(vmem_limit_bytes=mib * MIB)


def lists_kernel(me_ref, tile_ref, own_b, own_t, oth_b, oth_t):
    me = me_ref[0]

    def step(b, counts):
        own_n, oth_n = counts
        tile = tile_ref[b]
        own = (lax.shift_right_logical(tile, 8) == me).astype(jnp.int32)
        own_b[own_n] = b
        own_t[own_n] = tile
        oth_b[oth_n] = b
        oth_t[oth_n] = tile
        return own_n + own, oth_n + 1 - own

    lax.fori_loop(0, BLK, step, (jnp.int32(0), jnp.int32(0)))


def make_lists(me, block_tile):
    shape = jax.ShapeDtypeStruct((HALF_BLK + 1,), jnp.int32)
    return pl.pallas_call(
        lists_kernel,
        out_shape=(shape,) * 4,
        in_specs=[smem_spec()] * 2,
        out_specs=(smem_spec(),) * 4,
    )(me, block_tile)


def spread_kernel(pick, count, ssh, index, weight, wt_out, out):
    base = pl.program_id(0) * STEP
    lanes = lax.broadcasted_iota(jnp.int32, (4, BLOCK), 1)
    points = lax.broadcasted_iota(jnp.int32, (BLOCK, BLOCK), 0)

    def step(i, carry):
        b = pick[base + i]
        idx = index[b]
        wgt = jnp.where(lanes < count[b], weight[b], 0.0)
        mat = jnp.where(points == idx[0:1], wgt[0:1], 0.0)
        for k in range(1, 4):
            mat = mat + jnp.where(points == idx[k : k + 1], wgt[k : k + 1], 0.0)
        mat = mat.astype(BF16)
        wt_out[i] = mat
        heights = ssh[b]
        hi = heights.astype(BF16)
        lo = (heights - hi.astype(F32)).astype(BF16)
        both = lax.dot_general(
            jnp.concatenate([hi, lo], axis=0),
            mat,
            (((1,), (1,)), ((), ())),
            preferred_element_type=F32,
        )
        out[i] = (both[:NF] + both[NF:]).astype(out.dtype)
        return carry

    lax.fori_loop(0, STEP, step, 0, unroll=2)


def spread_half(pick, count, ssh, index, weight, dtype):
    return pl.pallas_call(
        spread_kernel,
        grid=(HALF_BLK // STEP,),
        out_shape=(
            jax.ShapeDtypeStruct((HALF_BLK, BLOCK, BLOCK), BF16),
            jax.ShapeDtypeStruct((HALF_BLK, NF, BLOCK), dtype),
        ),
        in_specs=[smem_spec(), smem_spec(), vmem_spec(), vmem_spec(), vmem_spec()],
        out_specs=(
            pl.BlockSpec((STEP, BLOCK, BLOCK), lambda i: (i, 0, 0)),
            pl.BlockSpec((STEP, NF, BLOCK), lambda i: (i, 0, 0)),
        ),
        compiler_params=params(24),
        cost_estimate=pl.CostEstimate(
            flops=2 * HALF_BLK * NF * BLOCK * BLOCK * 8, bytes_accessed=6 * MIB, transcendentals=0
        ),
    )(pick, count, ssh, index, weight)


def comp_re(u):
    return min(u, RADIX - u)


def comp_im(u):
    return 8 + min(u, RADIX - u)


def forward_kernel(
    me_ref, own_t, low_t, upp_t, own, low, upp, first, second, twc, tws, out, grid, mid, wide
):
    me = me_ref[0]
    flip = jnp.where(me >= DEVS // 2, 0xF0, 0)
    grid[...] = jnp.zeros_like(grid)

    def add_own(i, carry):
        tile = (own_t[i] & 255) ^ flip
        grid[tile] = grid[tile] + own[i]
        return carry

    lax.fori_loop(0, HALF_BLK, add_own, 0, unroll=2)

    def add_other(tiles, values):
        def body(i, carry):
            tile = tiles[i]
            mine = lax.shift_right_logical(tile, 8) == me
            spot = jnp.where(mine, (tile & 255) ^ flip, TILES)
            grid[spot] = grid[spot] + values[i].astype(F32)
            return carry

        lax.fori_loop(0, HALF_BLK, body, 0, unroll=2)

    add_other(low_t, low)
    add_other(upp_t, upp)

    def circle(r, carry):
        rows = grid[pl.ds(r * RADIX, RADIX)].reshape(RADIX * NF, BLOCK)
        hi = rows.astype(BF16)
        lo = (rows - hi.astype(F32)).astype(BF16)
        part = jnp.dot(first[...], hi, preferred_element_type=F32)
        comps = part[:256] + part[256:]
        comps = comps + jnp.dot(first[0:256], lo, preferred_element_type=F32)
        for u in range(RADIX):
            a = comps[comp_re(u) * NF : comp_re(u) * NF + NF]
            cu = twc[u : u + 1]
            su = tws[u : u + 1]
            if u == 0:
                re, im = a, jnp.zeros_like(a)
            elif u == 8:
                re, im = a * cu, -(a * su)
            else:
                b = comps[comp_im(u) * NF : comp_im(u) * NF + NF]
                if u < 8:
                    re, im = a * cu + b * su, b * cu - a * su
                else:
                    re, im = a * cu - b * su, -(b * cu + a * su)
            mid[u * NF : u * NF + NF, 0:BLOCK] = re.astype(BF16)
            mid[u * NF : u * NF + NF, BLOCK : 2 * BLOCK] = im.astype(BF16)
        res = lax.dot_general(
            second[...], mid[...], (((1,), (1,)), ((), ())), preferred_element_type=F32
        )
        res = res[:128] + res[128:]
        for c in range(2):
            for uh in range(2):
                wide[pl.ds(uh * 32 + c * 16 + r, NQ, stride=64), :] = res[
                    c * NQ : c * NQ + NQ, uh * 128 : uh * 128 + 128
                ]
        return carry

    lax.fori_loop(0, LAT, circle, 0)
    out[...] = wide[...].astype(BF16).reshape(out.shape)


def forward(me, own_t, low_t, upp_t, own, low, upp, tables):
    return pl.pallas_call(
        forward_kernel,
        out_shape=jax.ShapeDtypeStruct((DEVS, 32, 128), BF16),
        in_specs=[smem_spec()] * 4 + [vmem_spec()] * 7,
        out_specs=vmem_spec(),
        scratch_shapes=[
            VMEM((TILES + 1, NF, BLOCK), F32),
            VMEM((RADIX * NF, 2 * BLOCK), BF16),
            VMEM((DEVS * 32, 128), F32),
        ],
        compiler_params=params(32),
    )(
        me,
        own_t,
        low_t,
        upp_t,
        own,
        low,
        upp,
        tables["first"],
        tables["second"],
        tables["twc"],
        tables["tws"],
    )


def legendre_kernel(me_ref, table, data, gauss, love, out, ins, outs):
    k = pl.program_id(0)

    @pl.when(k == 0)
    def _():
        gw = gauss[...]
        for c in range(2):
            north = jnp.concatenate([data[i, c * 16 : c * 16 + 16] for i in range(64)], axis=0)
            south = jnp.concatenate(
                [data[127 - i, c * 16 : c * 16 + 16] for i in range(64)], axis=0
            )
            north = north.astype(F32).T
            south = south.astype(F32).T
            even = ((north + south) * gw).astype(BF16)
            odd = ((north - south) * gw).astype(BF16)
            ins[:, c * 16 : c * 16 + 16, :] = even.reshape(ORD, NF, NLAT)
            ins[:, 32 + c * 16 : 32 + c * 16 + 16, :] = odd.reshape(ORD, NF, NLAT)

    tab = table[0]
    both = jnp.dot(ins[k], tab, preferred_element_type=F32)
    order = me_ref[0] * ORD + k
    degree = lax.broadcasted_iota(jnp.int32, (32, NDEG), 1)
    is_even = ((degree + order) & 1) == 0
    coef = jnp.where(is_even, both[:32], both[32:])
    coef = jnp.where(degree < order, 0.0, coef)
    coef = coef * love[...]
    parts = jnp.concatenate(
        [jnp.where(is_even, coef, 0.0), jnp.where(is_even, 0.0, coef)], axis=0
    ).astype(BF16)
    res = lax.dot_general(parts, tab, (((1,), (1,)), ((), ())), preferred_element_type=F32)
    upper = res[:32] + res[32:]
    lower = res[:32] - res[32:]
    spot = pl.ds(pl.multiple_of(k * NF, NF), NF)
    for c in range(2):
        outs[c, 0, spot, :] = upper[c * 16 : c * 16 + 16]
        outs[c, 1, spot, :] = lower[c * 16 : c * 16 + 16]

    @pl.when(k == ORD - 1)
    def _():
        for c in range(2):
            up = outs[c, 0].T.astype(BF16)
            dn = outs[c, 1].T.astype(BF16)
            for i in range(64):
                out[i, c * 16 : c * 16 + 16] = up[i * 16 : i * 16 + 16]
                out[127 - i, c * 16 : c * 16 + 16] = dn[i * 16 : i * 16 + 16]


def legendre_both(me, table, data, gauss, love):
    return pl.pallas_call(
        legendre_kernel,
        grid=(ORD,),
        out_shape=jax.ShapeDtypeStruct((DEVS, 32, 128), BF16),
        in_specs=[
            smem_spec(),
            pl.BlockSpec((1, NLAT, NDEG), lambda k: (k, 0, 0)),
            vmem_spec(),
            vmem_spec(),
            vmem_spec(),
        ],
        out_specs=pl.BlockSpec((DEVS, 32, 128), lambda k: (0, 0, 0)),
        scratch_shapes=[VMEM((ORD, 64, NLAT), BF16), VMEM((2, 2, 128, NLAT), F32)],
        compiler_params=params(40),
    )(me, table, data, gauss.reshape(1, NLAT), love.reshape(1, NDEG))


def inverse_kernel(
    me_ref, own_t, low_t, upp_t, data, second, last, twc, tws, own, low, upp, wide, tiles, mid
):
    me = me_ref[0]
    flip = jnp.where(me >= DEVS // 2, 0xF0, 0)
    wide[...] = data[...].astype(F32).reshape(wide.shape)
    row = lax.broadcasted_iota(jnp.int32, (NQ, 128), 0)
    lane = lax.broadcasted_iota(jnp.int32, (NQ, 128), 1)
    zonal = jnp.where((row == 0) & (lane < NF), 0.5, 1.0)

    def circle(r, carry):
        parts = []
        for c in range(2):
            left = wide[pl.ds(c * 16 + r, NQ, stride=64), :] * zonal
            right = wide[pl.ds(32 + c * 16 + r, NQ, stride=64), :]
            parts.append(jnp.concatenate([left, right], axis=1))
        spectrum = jnp.concatenate(parts, axis=0).T.astype(BF16)
        spectrum = jnp.concatenate([spectrum, spectrum], axis=1)
        waves = jnp.dot(spectrum, second[...], preferred_element_type=F32)
        res, ims = {}, {}
        for u in range(RADIX):
            a = waves[u * NF : u * NF + NF, 0:BLOCK]
            b = waves[u * NF : u * NF + NF, BLOCK : 2 * BLOCK]
            cu = twc[u : u + 1]
            su = tws[u : u + 1]
            res[u] = a * cu - b * su if u else a
            if u not in (0, 8):
                ims[u] = a * su + b * cu
        for u in range(9):
            val = res[u] if u in (0, 8) else res[u] + res[RADIX - u]
            mid[u * NF : u * NF + NF] = val.astype(BF16)
        for u in range(1, 8):
            val = ims[u] - ims[RADIX - u]
            mid[(8 + u) * NF : (8 + u) * NF + NF] = val.astype(BF16)
        comps = mid[...]
        load = jnp.dot(last[:, 0:256], comps, preferred_element_type=F32)
        load = load + jnp.dot(last[:, 256:512], comps, preferred_element_type=F32)
        tiles[pl.ds(r * RADIX, RADIX)] = load.reshape(RADIX, NF, BLOCK)
        return carry

    lax.fori_loop(0, LAT, circle, 0)

    def gather(i, carry):
        own[i] = tiles[(own_t[i] & 255) ^ flip]
        low[i] = tiles[(low_t[i] & 255) ^ flip].astype(BF16)
        upp[i] = tiles[(upp_t[i] & 255) ^ flip].astype(BF16)
        return carry

    lax.fori_loop(0, HALF_BLK, gather, 0, unroll=2)


def inverse(me, own_t, low_t, upp_t, data, tables):
    return pl.pallas_call(
        inverse_kernel,
        out_shape=(
            jax.ShapeDtypeStruct((HALF_BLK, NF, BLOCK), F32),
            jax.ShapeDtypeStruct((HALF_BLK, NF, BLOCK), BF16),
            jax.ShapeDtypeStruct((HALF_BLK, NF, BLOCK), BF16),
        ),
        in_specs=[smem_spec()] * 4 + [vmem_spec()] * 5,
        out_specs=(vmem_spec(),) * 3,
        scratch_shapes=[
            VMEM((DEVS * 32, 128), F32),
            VMEM((TILES, NF, BLOCK), F32),
            VMEM((RADIX * NF, BLOCK), BF16),
        ],
        compiler_params=params(32),
    )(
        me,
        own_t,
        low_t,
        upp_t,
        data,
        tables["second"],
        tables["last"],
        tables["twc"],
        tables["tws"],
    )


def own_kernel(values, wt, out):
    for i in range(STEP):
        val = values[i]
        hi = val.astype(BF16)
        lo = (val - hi.astype(F32)).astype(BF16)
        both = jnp.dot(jnp.concatenate([hi, lo], axis=0), wt[i], preferred_element_type=F32)
        out[i] = both[:NF] + both[NF:]


def own_cells(values, wt):
    return pl.pallas_call(
        own_kernel,
        grid=(HALF_BLK // STEP,),
        out_shape=jax.ShapeDtypeStruct((HALF_BLK, NF, BLOCK), F32),
        in_specs=[
            pl.BlockSpec((STEP, NF, BLOCK), lambda i: (i, 0, 0)),
            pl.BlockSpec((STEP, BLOCK, BLOCK), lambda i: (i, 0, 0)),
        ],
        out_specs=pl.BlockSpec((STEP, NF, BLOCK), lambda i: (i, 0, 0)),
        compiler_params=params(16),
        cost_estimate=pl.CostEstimate(
            flops=2 * HALF_BLK * NF * BLOCK * BLOCK * 4, bytes_accessed=5 * MIB, transcendentals=0
        ),
    )(values, wt)


def cells_kernel(me_ref, own_b, oth_b, oth_t, own, low, upp, wt, out):
    me = me_ref[0]
    step_id = pl.program_id(0)

    @pl.when(step_id == 0)
    def _():
        def copy(i, carry):
            out[own_b[i]] = own[i]
            return carry

        lax.fori_loop(0, HALF_BLK, copy, 0, unroll=2)

    for i in range(STEP):
        slot = step_id * STEP + i
        above = lax.shift_right_logical(oth_t[slot], 8) > me
        val = jnp.where(above, upp[slot], low[slot])
        out[oth_b[slot]] = jnp.dot(val, wt[i], preferred_element_type=F32)


def all_cells(me, own_b, oth_b, oth_t, own, low, upp, wt):
    return pl.pallas_call(
        cells_kernel,
        grid=(HALF_BLK // STEP,),
        out_shape=jax.ShapeDtypeStruct((BLK, NF, BLOCK), F32),
        in_specs=[smem_spec()] * 4
        + [vmem_spec()] * 3
        + [pl.BlockSpec((STEP, BLOCK, BLOCK), lambda i: (i, 0, 0))],
        out_specs=pl.BlockSpec((BLK, NF, BLOCK), lambda i: (0, 0, 0)),
        compiler_params=params(16),
    )(me, own_b, oth_b, oth_t, own, low, upp, wt)


def shift(value, steps):
    pairs = [(source, (source + steps) % DEVS) for source in range(DEVS)]
    return lax.ppermute(value, AXES, pairs)


def on_device(
    tables, ssh, cell_count, remap_index, remap_weight, block_tile, gauss_weight, love, legendre
):
    rank = lax.axis_index(AXES).astype(jnp.int32)
    me = rank.reshape(1)
    own_b, own_t, oth_b, oth_t = make_lists(me, block_tile)
    low_t = shift(oth_t, 1)
    upp_t = shift(oth_t, -1)
    wt_oth, oth = spread_half(oth_b, cell_count, ssh, remap_index, remap_weight, BF16)
    low = shift(oth, 1)
    upp = shift(oth, -1)
    wt_own, own = spread_half(own_b, cell_count, ssh, remap_index, remap_weight, F32)
    fourier = forward(me, own_t, low_t, upp_t, own, low, upp, tables)
    by_order = lax.all_to_all(fourier, AXES, split_axis=0, concat_axis=0, tiled=True)
    synth = legendre_both(me, legendre, by_order, gauss_weight, love)
    by_lat = lax.all_to_all(synth, AXES, split_axis=0, concat_axis=0, tiled=True)
    own_v, low_v, upp_v = inverse(me, own_t, low_t, upp_t, by_lat, tables)
    from_low = shift(upp_v, 1)
    from_upp = shift(low_v, -1)
    own_cell = own_cells(own_v, wt_own)
    return all_cells(me, own_b, oth_b, oth_t, own_cell, from_low, from_upp, wt_oth)


def solution(mesh):
    tables = {name: jnp.asarray(table) for name, table in make_tables().items()}
    return jax.shard_map(
        functools.partial(on_device, tables),
        mesh=mesh,
        in_specs=(
            P(AXES, None, None),
            P(AXES),
            P(AXES, None, None),
            P(AXES, None, None),
            P(AXES),
            P(),
            P(),
            P(AXES, None, None),
        ),
        out_specs=P(AXES, None, None),
        check_vma=False,
    )
```

```python
import functools
import math

import jax
import jax.numpy as jnp
import numpy as np
from jax import lax
from jax.experimental import pallas as pl
from jax.experimental.pallas import tpu as pltpu
from jax.sharding import PartitionSpec as P

AXES = ("dom", "order")
DEVS = 128
NF = 16
BLOCK = 256
BLK = 64
HALF_BLK = 32
TILES = 256
LAT = 16
ORD = 8
NLAT = 1024
NDEG = 1024
RADIX = 16
NQ = 64
STEP = 8
F32 = jnp.float32
BF16 = jnp.bfloat16
MIB = 1 << 20

SMEM = pltpu.SMEM
VMEM = pltpu.VMEM


def hi_lo(table):
    table = np.asarray(table, np.float32)
    hi = table.astype(jnp.bfloat16)
    lo = (table - hi.astype(np.float32)).astype(jnp.bfloat16)
    return hi, lo


def make_tables():
    points = np.arange(BLOCK)
    angle = 2 * np.pi * ((np.arange(NQ)[:, None] * points[None, :]) % BLOCK) / BLOCK
    cos, sin = np.cos(angle), np.sin(angle)
    second = np.concatenate(
        [np.concatenate([cos, sin], axis=1), np.concatenate([-sin, cos], axis=1)], axis=0
    )
    s_hi, s_lo = hi_lo(second)
    twist = 2 * np.pi * (np.arange(RADIX)[:, None] * points[None, :]) / 4096.0
    return dict(
        second=np.concatenate([s_hi, s_lo], axis=0),
        twc=np.cos(twist).astype(np.float32),
        tws=np.sin(twist).astype(np.float32),
    )


ROOT = math.sqrt(0.5)
COS1 = math.cos(math.pi / 8)
SIN1 = math.sin(math.pi / 8)


def real_dft16(g):
    e = [g[s] + g[s + 8] for s in range(8)]
    o = [g[s] - g[s + 8] for s in range(8)]
    re, im = [None] * 9, [None] * 9
    ee = [e[s] + e[s + 4] for s in range(4)]
    eo = [e[s] - e[s + 4] for s in range(4)]
    x, y = ee[0] + ee[2], ee[1] + ee[3]
    re[0], re[8] = x + y, x - y
    re[4], im[4] = ee[0] - ee[2], ee[3] - ee[1]

    def odd4(p):
        d, s = (p[1] - p[3]) * ROOT, (p[1] + p[3]) * ROOT
        return (p[0] + d, -(s + p[2])), (p[0] - d, p[2] - s)

    (re[2], im[2]), (re[6], im[6]) = odd4(eo)
    a1, a3 = odd4(o[0::2])
    b1, b3 = odd4(o[1::2])
    t = (b1[0] * COS1 + b1[1] * SIN1, b1[1] * COS1 - b1[0] * SIN1)
    re[1], im[1] = a1[0] + t[0], a1[1] + t[1]
    re[7], im[7] = a1[0] - t[0], t[1] - a1[1]
    t = (b3[0] * SIN1 + b3[1] * COS1, b3[1] * SIN1 - b3[0] * COS1)
    re[3], im[3] = a3[0] + t[0], a3[1] + t[1]
    re[5], im[5] = a3[0] - t[0], t[1] - a3[1]
    return re, im


def real_idft16(a, b):
    x, z = a[0] + a[8], a[0] - a[8]
    q = [x + a[4], z - b[4], x - a[4], z + b[4]]

    def odd4(p1, p3):
        d, s = (p1[0] - p3[0]) * ROOT, (p1[1] + p3[1]) * ROOT
        return [p1[0] + p3[0], d - s, p3[1] - p1[1], -(d + s)]

    w = odd4((a[2], b[2]), (a[6], b[6]))
    even = [q[t] + w[t] for t in range(4)] + [q[t] - w[t] for t in range(4)]
    p1, q1 = (a[1] + a[7], b[1] - b[7]), (a[1] - a[7], b[1] + b[7])
    p3, q3 = (a[3] + a[5], b[3] - b[5]), (a[3] - a[5], b[3] + b[5])
    q1 = (q1[0] * COS1 - q1[1] * SIN1, q1[0] * SIN1 + q1[1] * COS1)
    q3 = (q3[0] * SIN1 - q3[1] * COS1, q3[0] * COS1 + q3[1] * SIN1)
    oe, oo = odd4(p1, p3), odd4(q1, q3)
    odd = [oe[s // 2] if s % 2 == 0 else oo[s // 2] for s in range(8)]
    return [even[s] + odd[s] for s in range(8)] + [even[s] - odd[s] for s in range(8)]


def vmem_spec():
    return pl.BlockSpec(memory_space=VMEM)


def smem_spec():
    return pl.BlockSpec(memory_space=SMEM)


def plain_spec():
    return pl.BlockSpec()


def cost(micros):
    return pl.CostEstimate(flops=micros * 10**9, bytes_accessed=4 * MIB, transcendentals=0)


def params(mib):
    return pltpu.CompilerParams(vmem_limit_bytes=mib * MIB)


OWN_B, OWN_T, OTH_B, OTH_T, COUNT, LISTS = 0, 40, 80, 120, 160, 224


def make_lists(tile_ref, count_ref, lists):
    me = lax.axis_index(AXES)

    def step(b, counts):
        own_n, oth_n = counts
        tile = tile_ref[b]
        own = (lax.shift_right_logical(tile, 8) == me).astype(jnp.int32)
        lists[OWN_B + own_n] = b
        lists[OWN_T + own_n] = tile
        lists[OTH_B + oth_n] = b
        lists[OTH_T + oth_n] = tile
        lists[COUNT + b] = count_ref[b]
        return own_n + own, oth_n + 1 - own

    lax.fori_loop(0, BLK, step, (jnp.int32(0), jnp.int32(0)), unroll=4)


def spread_blocks(first, lists, ssh, index, weight, wt_out, out):
    base = pl.program_id(0) * STEP
    lanes = lax.broadcasted_iota(jnp.int32, (4, BLOCK), 1)
    points = lax.broadcasted_iota(jnp.int32, (BLOCK, BLOCK), 0).astype(F32).astype(BF16)
    zero = jnp.bfloat16(0)
    for i in range(STEP):
        b = lists[first + base + i]
        idx = index[b].astype(F32).astype(BF16)
        wgt = jnp.where(lanes < lists[COUNT + b], weight[b], 0.0).astype(BF16)
        mat = jnp.where(points == idx[0:1], wgt[0:1], zero)
        for k in range(1, 4):
            mat = mat + jnp.where(points == idx[k : k + 1], wgt[k : k + 1], zero)
        wt_out[i] = mat
        heights = ssh[b]
        hi = heights.astype(BF16)
        lo = (heights - hi.astype(F32)).astype(BF16)
        both = lax.dot_general(
            jnp.concatenate([hi, lo], axis=0),
            mat,
            (((1,), (1,)), ((), ())),
            preferred_element_type=F32,
        )
        out[i] = (both[:NF] + both[NF:]).astype(out.dtype)


def other_kernel(
    tile_hbm, count_hbm, ssh_hbm, index_hbm, weight_hbm, lists, wt_out, out,
    tile_ref, count_ref, ssh, index, weight, sems
):
    @pl.when(pl.program_id(0) == 0)
    def _():
        pairs = [
            (tile_hbm, tile_ref),
            (count_hbm, count_ref),
            (index_hbm, index),
            (weight_hbm, weight),
            (ssh_hbm, ssh),
        ]
        copies = [pltpu.make_async_copy(s, d, sems.at[i]) for i, (s, d) in enumerate(pairs)]
        for copy in copies:
            copy.start()
        copies[0].wait()
        copies[1].wait()
        make_lists(tile_ref, count_ref, lists)
        for copy in copies[2:]:
            copy.wait()

    spread_blocks(OTH_B, lists, ssh, index, weight, wt_out, out)


def own_spread_kernel(lists, ssh, index, weight, wt_out, out):
    spread_blocks(OWN_B, lists, ssh, index, weight, wt_out, out)


def whole(shape):
    return pl.BlockSpec(shape, lambda i: (0,) * len(shape))


def spread_half(scalars, ssh, index, weight, dtype, with_lists):
    shapes = (
        jax.ShapeDtypeStruct((HALF_BLK, BLOCK, BLOCK), BF16),
        jax.ShapeDtypeStruct((HALF_BLK, NF, BLOCK), dtype),
    )
    specs = (
        pl.BlockSpec((STEP, BLOCK, BLOCK), lambda i: (i, 0, 0)),
        pl.BlockSpec((STEP, NF, BLOCK), lambda i: (i, 0, 0)),
    )
    if with_lists:
        shapes = (jax.ShapeDtypeStruct((LISTS,), jnp.int32),) + shapes
        specs = (smem_spec(),) + specs
        in_specs = [pl.BlockSpec(memory_space=pltpu.HBM)] * 5
        scratch = [
            SMEM((BLK,), jnp.int32),
            SMEM((BLK,), jnp.int32),
            VMEM((BLK, NF, BLOCK), F32),
            VMEM((BLK, 4, BLOCK), jnp.int32),
            VMEM((BLK, 4, BLOCK), F32),
            pltpu.SemaphoreType.DMA((5,)),
        ]
    else:
        in_specs = [
            smem_spec(),
            whole((BLK, NF, BLOCK)),
            whole((BLK, 4, BLOCK)),
            whole((BLK, 4, BLOCK)),
        ]
        scratch = []
    return pl.pallas_call(
        other_kernel if with_lists else own_spread_kernel,
        grid=(HALF_BLK // STEP,),
        out_shape=shapes,
        in_specs=in_specs,
        out_specs=specs,
        scratch_shapes=scratch,
        compiler_params=params(14),
        cost_estimate=cost(5),
    )(*scalars, ssh, index, weight)


def forward_kernel(lists, low_t, upp_t, own, low, upp, second, twc, tws, out, grid, mid, wide):
    me = lax.axis_index(AXES)
    flip = jnp.where(me >= DEVS // 2, 0xF0, 0)
    grid[...] = jnp.zeros_like(grid)

    def add_own(i, carry):
        tile = (lists[OWN_T + i] & 255) ^ flip
        grid[tile] = grid[tile] + own[i]
        return carry

    lax.fori_loop(0, HALF_BLK, add_own, 0, unroll=4)

    def add_other(tiles, values):
        def body(i, carry):
            tile = tiles[OTH_T + i]
            mine = lax.shift_right_logical(tile, 8) == me
            spot = jnp.where(mine, (tile & 255) ^ flip, TILES)
            grid[spot] = grid[spot] + values[i].astype(F32)
            return carry

        lax.fori_loop(0, HALF_BLK, body, 0, unroll=4)

    add_other(low_t, low)
    add_other(upp_t, upp)

    def circle(r, carry):
        for h in range(2):
            lanes = slice(h * 128, h * 128 + 128)
            re, im = real_dft16([grid[r * RADIX + s, :, lanes] for s in range(RADIX)])
            for u in range(RADIX):
                v = min(u, RADIX - u)
                cu, su = twc[u : u + 1, lanes], tws[u : u + 1, lanes]
                if u == 0:
                    x, y = re[0], jnp.zeros_like(re[0])
                elif u == 8:
                    x, y = re[8] * cu, -(re[8] * su)
                elif u < 8:
                    x, y = re[v] * cu + im[v] * su, im[v] * cu - re[v] * su
                else:
                    x, y = re[v] * cu - im[v] * su, -(im[v] * cu + re[v] * su)
                rows = slice(u * NF, u * NF + NF)
                mid[r, rows, h * 128 : h * 128 + 128] = x.astype(BF16)
                mid[r, rows, 256 + h * 128 : 256 + h * 128 + 128] = y.astype(BF16)
        return carry

    lax.fori_loop(0, LAT, circle, 0, unroll=2)
    for r in range(LAT):
        res = lax.dot_general(
            second[...], mid[r], (((1,), (1,)), ((), ())), preferred_element_type=F32
        )
        res = (res[:128] + res[128:]) * (1.0 / 4096.0)
        for c in range(2):
            for uh in range(2):
                wide[pl.ds(uh * 32 + c * 16 + r, NQ, stride=64), :] = res[
                    c * NQ : c * NQ + NQ, uh * 128 : uh * 128 + 128
                ]
    out[...] = wide[...].astype(BF16).reshape(out.shape)


def forward(lists, low_t, upp_t, own, low, upp, tables):
    return pl.pallas_call(
        forward_kernel,
        out_shape=jax.ShapeDtypeStruct((DEVS, 32, 128), BF16),
        in_specs=[smem_spec()] * 3 + [vmem_spec()] * 3 + [plain_spec()] * 3,
        out_specs=vmem_spec(),
        scratch_shapes=[
            VMEM((TILES + 1, NF, BLOCK), F32),
            VMEM((LAT, RADIX * NF, 2 * BLOCK), BF16),
            VMEM((DEVS * 32, 128), F32),
        ],
        compiler_params=params(18),
        cost_estimate=cost(8),
    )(lists, low_t, upp_t, own, low, upp, tables["second"], tables["twc"], tables["tws"])


def legendre_kernel(table, data, gauss, love, out, ins, outs):
    first_order = lax.axis_index(AXES) * ORD
    gw = gauss[...]
    for c in range(2):
        north = jnp.concatenate([data[i, c * 16 : c * 16 + 16] for i in range(64)], axis=0)
        south = jnp.concatenate([data[127 - i, c * 16 : c * 16 + 16] for i in range(64)], axis=0)
        north = north.astype(F32).T
        south = south.astype(F32).T
        even = ((north + south) * gw).astype(BF16)
        odd = ((north - south) * gw).astype(BF16)
        ins[:, c * 16 : c * 16 + 16, :] = even.reshape(ORD, NF, NLAT)
        ins[:, 32 + c * 16 : 32 + c * 16 + 16, :] = odd.reshape(ORD, NF, NLAT)
    degree = lax.broadcasted_iota(jnp.int32, (32, NDEG), 1)
    for k in range(ORD):
        both = jnp.dot(ins[k], table[k], preferred_element_type=F32)
        order = first_order + k
        is_even = ((degree + order) & 1) == 0
        coef = jnp.where(is_even, both[:32], both[32:])
        coef = jnp.where(degree < order, 0.0, coef)
        coef = coef * love[...]
        parts = jnp.concatenate(
            [jnp.where(is_even, coef, 0.0), jnp.where(is_even, 0.0, coef)], axis=0
        ).astype(BF16)
        res = lax.dot_general(
            parts, table[k], (((1,), (1,)), ((), ())), preferred_element_type=F32
        )
        upper = res[:32] + res[32:]
        lower = res[:32] - res[32:]
        for c in range(2):
            outs[c, 0, k * NF : k * NF + NF, :] = upper[c * 16 : c * 16 + 16]
            outs[c, 1, k * NF : k * NF + NF, :] = lower[c * 16 : c * 16 + 16]
    for c in range(2):
        up = outs[c, 0].T.astype(BF16)
        dn = outs[c, 1].T.astype(BF16)
        for i in range(64):
            out[i, c * 16 : c * 16 + 16] = up[i * 16 : i * 16 + 16]
            out[127 - i, c * 16 : c * 16 + 16] = dn[i * 16 : i * 16 + 16]


def legendre_both(table, data, gauss, love):
    return pl.pallas_call(
        legendre_kernel,
        out_shape=jax.ShapeDtypeStruct((DEVS, 32, 128), BF16),
        in_specs=[plain_spec(), vmem_spec(), plain_spec(), plain_spec()],
        out_specs=vmem_spec(),
        scratch_shapes=[VMEM((ORD, 64, NLAT), BF16), VMEM((2, 2, 128, NLAT), F32)],
        compiler_params=params(12),
        cost_estimate=cost(11),
    )(table, data, gauss.reshape(1, NLAT), love.reshape(1, NDEG))


def inverse_kernel(
    lists, low_t, upp_t, data, second, twc, tws, own, low, upp, wide, tiles, waves
):
    me = lax.axis_index(AXES)
    flip = jnp.where(me >= DEVS // 2, 0xF0, 0)
    wide[...] = data[...].astype(F32).reshape(wide.shape)
    row = lax.broadcasted_iota(jnp.int32, (NQ, 128), 0)
    lane = lax.broadcasted_iota(jnp.int32, (NQ, 128), 1)
    zonal = jnp.where((row == 0) & (lane < NF), 1.0, 2.0)
    for r in range(LAT):
        parts = []
        for c in range(2):
            left = wide[pl.ds(c * 16 + r, NQ, stride=64), :] * zonal
            right = wide[pl.ds(32 + c * 16 + r, NQ, stride=64), :] * 2.0
            parts.append(jnp.concatenate([left, right], axis=1))
        spectrum = jnp.concatenate(parts, axis=0).T.astype(BF16)
        spectrum = jnp.concatenate([spectrum, spectrum], axis=1)
        waves[r] = jnp.dot(spectrum, second[...], preferred_element_type=F32)

    def circle(r, carry):
        for h in range(2):
            lanes = slice(h * 128, h * 128 + 128)
            re, im = {}, {}
            for u in range(RADIX):
                rows = slice(u * NF, u * NF + NF)
                x = waves[r, rows, h * 128 : h * 128 + 128]
                y = waves[r, rows, 256 + h * 128 : 256 + h * 128 + 128]
                cu, su = twc[u : u + 1, lanes], tws[u : u + 1, lanes]
                re[u] = x * cu - y * su if u else x
                if u not in (0, 8):
                    im[u] = x * su + y * cu
            a = [re[0]] + [re[u] + re[RADIX - u] for u in range(1, 8)] + [re[8]]
            b = [None] + [im[u] - im[RADIX - u] for u in range(1, 8)]
            values = real_idft16(a, b)
            for s in range(RADIX):
                tiles[r * RADIX + s, :, lanes] = values[s]
        return carry

    lax.fori_loop(0, LAT, circle, 0)

    def gather(i, carry):
        own[i] = tiles[(lists[OWN_T + i] & 255) ^ flip]
        low[i] = tiles[(low_t[OTH_T + i] & 255) ^ flip].astype(BF16)
        upp[i] = tiles[(upp_t[OTH_T + i] & 255) ^ flip].astype(BF16)
        return carry

    lax.fori_loop(0, HALF_BLK, gather, 0, unroll=4)


def inverse(lists, low_t, upp_t, data, tables):
    return pl.pallas_call(
        inverse_kernel,
        out_shape=(
            jax.ShapeDtypeStruct((HALF_BLK, NF, BLOCK), F32),
            jax.ShapeDtypeStruct((HALF_BLK, NF, BLOCK), BF16),
            jax.ShapeDtypeStruct((HALF_BLK, NF, BLOCK), BF16),
        ),
        in_specs=[smem_spec()] * 3 + [vmem_spec()] + [plain_spec()] * 3,
        out_specs=(vmem_spec(),) * 3,
        scratch_shapes=[
            VMEM((DEVS * 32, 128), F32),
            VMEM((TILES, NF, BLOCK), F32),
            VMEM((LAT, RADIX * NF, 2 * BLOCK), F32),
        ],
        compiler_params=params(20),
        cost_estimate=cost(7),
    )(lists, low_t, upp_t, data, tables["second"], tables["twc"], tables["tws"])


def own_kernel(values, wt, out):
    for i in range(STEP):
        val = values[i]
        hi = val.astype(BF16)
        lo = (val - hi.astype(F32)).astype(BF16)
        both = jnp.dot(jnp.concatenate([hi, lo], axis=0), wt[i], preferred_element_type=F32)
        out[i] = both[:NF] + both[NF:]


def own_cells(values, wt):
    return pl.pallas_call(
        own_kernel,
        grid=(HALF_BLK // STEP,),
        out_shape=jax.ShapeDtypeStruct((HALF_BLK, NF, BLOCK), F32),
        in_specs=[
            pl.BlockSpec((STEP, NF, BLOCK), lambda i: (i, 0, 0)),
            pl.BlockSpec((STEP, BLOCK, BLOCK), lambda i: (i, 0, 0)),
        ],
        out_specs=pl.BlockSpec((STEP, NF, BLOCK), lambda i: (i, 0, 0)),
        compiler_params=params(8),
        cost_estimate=cost(2),
    )(values, wt)


def cells_kernel(lists, own, low, upp, wt, out):
    me = lax.axis_index(AXES)
    step_id = pl.program_id(0)

    @pl.when(step_id == 0)
    def _():
        def copy(i, carry):
            out[lists[OWN_B + i]] = own[i]
            return carry

        lax.fori_loop(0, HALF_BLK, copy, 0, unroll=2)

    for i in range(STEP):
        slot = step_id * STEP + i
        above = lax.shift_right_logical(lists[OTH_T + slot], 8) > me
        val = jnp.where(above, upp[slot], low[slot])
        out[lists[OTH_B + slot]] = jnp.dot(val, wt[i], preferred_element_type=F32)


def all_cells(lists, own, low, upp, wt):
    return pl.pallas_call(
        cells_kernel,
        grid=(HALF_BLK // STEP,),
        out_shape=jax.ShapeDtypeStruct((BLK, NF, BLOCK), F32),
        in_specs=[smem_spec()]
        + [vmem_spec()] * 3
        + [pl.BlockSpec((STEP, BLOCK, BLOCK), lambda i: (i, 0, 0))],
        out_specs=pl.BlockSpec((BLK, NF, BLOCK), lambda i: (0, 0, 0)),
        compiler_params=params(8),
        cost_estimate=cost(4),
    )(lists, own, low, upp, wt)


def shift(value, steps):
    pairs = [(source, (source + steps) % DEVS) for source in range(DEVS)]
    return lax.ppermute(value, AXES, pairs)


def on_device(
    tables, ssh, cell_count, remap_index, remap_weight, block_tile, gauss_weight, love, legendre
):
    lists, wt_oth, oth = spread_half(
        (block_tile, cell_count), ssh, remap_index, remap_weight, BF16, True
    )
    low_t = shift(lists, 1)
    upp_t = shift(lists, -1)
    low = shift(oth, 1)
    upp = shift(oth, -1)
    wt_own, own = spread_half((lists,), ssh, remap_index, remap_weight, F32, False)
    fourier = forward(lists, low_t, upp_t, own, low, upp, tables)
    by_order = lax.all_to_all(fourier, AXES, split_axis=0, concat_axis=0, tiled=True)
    synth = legendre_both(legendre, by_order, gauss_weight, love)
    by_lat = lax.all_to_all(synth, AXES, split_axis=0, concat_axis=0, tiled=True)
    own_v, low_v, upp_v = inverse(lists, low_t, upp_t, by_lat, tables)
    from_low = shift(upp_v, 1)
    from_upp = shift(low_v, -1)
    own_cell = own_cells(own_v, wt_own)
    return all_cells(lists, own_cell, from_low, from_upp, wt_oth)


def solution(mesh):
    tables = {name: jnp.asarray(table) for name, table in make_tables().items()}
    return jax.shard_map(
        functools.partial(on_device, tables),
        mesh=mesh,
        in_specs=(
            P(AXES, None, None),
            P(AXES),
            P(AXES, None, None),
            P(AXES, None, None),
            P(AXES),
            P(),
            P(),
            P(AXES, None, None),
        ),
        out_specs=P(AXES, None, None),
        check_vma=False,
    )
```

```python
import functools
import math

import jax
import jax.numpy as jnp
import numpy as np
from jax import lax
from jax.experimental import pallas as pl
from jax.experimental.pallas import tpu as pltpu
from jax.sharding import PartitionSpec as P

AXES = ("dom", "order")
DEVS = 128
NF = 16
BLOCK = 256
BLK = 64
HALF_BLK = 32
TILES = 256
LAT = 16
ORD = 8
NLAT = 1024
NDEG = 1024
RADIX = 16
NQ = 64
STEP = 8
F32 = jnp.float32
BF16 = jnp.bfloat16
MIB = 1 << 20

SMEM = pltpu.SMEM
VMEM = pltpu.VMEM


def hi_lo(table):
    table = np.asarray(table, np.float32)
    hi = table.astype(jnp.bfloat16)
    lo = (table - hi.astype(np.float32)).astype(jnp.bfloat16)
    return hi, lo


def make_tables():
    points = np.arange(BLOCK)
    angle = 2 * np.pi * ((np.arange(NQ)[:, None] * points[None, :]) % BLOCK) / BLOCK
    cos, sin = np.cos(angle), np.sin(angle)
    second = np.concatenate(
        [np.concatenate([cos, sin], axis=1), np.concatenate([-sin, cos], axis=1)], axis=0
    )
    s_hi, s_lo = hi_lo(second)
    twist = 2 * np.pi * (np.arange(RADIX)[:, None] * points[None, :]) / 4096.0
    return dict(
        second=np.concatenate([s_hi, s_lo], axis=0),
        twc=np.cos(twist).astype(np.float32),
        tws=np.sin(twist).astype(np.float32),
    )


ROOT = math.sqrt(0.5)
COS1 = math.cos(math.pi / 8)
SIN1 = math.sin(math.pi / 8)


def real_dft16(g):
    e = [g[s] + g[s + 8] for s in range(8)]
    o = [g[s] - g[s + 8] for s in range(8)]
    re, im = [None] * 9, [None] * 9
    ee = [e[s] + e[s + 4] for s in range(4)]
    eo = [e[s] - e[s + 4] for s in range(4)]
    x, y = ee[0] + ee[2], ee[1] + ee[3]
    re[0], re[8] = x + y, x - y
    re[4], im[4] = ee[0] - ee[2], ee[3] - ee[1]

    def odd4(p):
        d, s = (p[1] - p[3]) * ROOT, (p[1] + p[3]) * ROOT
        return (p[0] + d, -(s + p[2])), (p[0] - d, p[2] - s)

    (re[2], im[2]), (re[6], im[6]) = odd4(eo)
    a1, a3 = odd4(o[0::2])
    b1, b3 = odd4(o[1::2])
    t = (b1[0] * COS1 + b1[1] * SIN1, b1[1] * COS1 - b1[0] * SIN1)
    re[1], im[1] = a1[0] + t[0], a1[1] + t[1]
    re[7], im[7] = a1[0] - t[0], t[1] - a1[1]
    t = (b3[0] * SIN1 + b3[1] * COS1, b3[1] * SIN1 - b3[0] * COS1)
    re[3], im[3] = a3[0] + t[0], a3[1] + t[1]
    re[5], im[5] = a3[0] - t[0], t[1] - a3[1]
    return re, im


def real_idft16(a, b):
    x, z = a[0] + a[8], a[0] - a[8]
    q = [x + a[4], z - b[4], x - a[4], z + b[4]]

    def odd4(p1, p3):
        d, s = (p1[0] - p3[0]) * ROOT, (p1[1] + p3[1]) * ROOT
        return [p1[0] + p3[0], d - s, p3[1] - p1[1], -(d + s)]

    w = odd4((a[2], b[2]), (a[6], b[6]))
    even = [q[t] + w[t] for t in range(4)] + [q[t] - w[t] for t in range(4)]
    p1, q1 = (a[1] + a[7], b[1] - b[7]), (a[1] - a[7], b[1] + b[7])
    p3, q3 = (a[3] + a[5], b[3] - b[5]), (a[3] - a[5], b[3] + b[5])
    q1 = (q1[0] * COS1 - q1[1] * SIN1, q1[0] * SIN1 + q1[1] * COS1)
    q3 = (q3[0] * SIN1 - q3[1] * COS1, q3[0] * COS1 + q3[1] * SIN1)
    oe, oo = odd4(p1, p3), odd4(q1, q3)
    odd = [oe[s // 2] if s % 2 == 0 else oo[s // 2] for s in range(8)]
    return [even[s] + odd[s] for s in range(8)] + [even[s] - odd[s] for s in range(8)]


def vmem_spec():
    return pl.BlockSpec(memory_space=VMEM)


def smem_spec():
    return pl.BlockSpec(memory_space=SMEM)


def plain_spec():
    return pl.BlockSpec()


def cost(micros):
    return pl.CostEstimate(flops=micros * 10**9, bytes_accessed=4 * MIB, transcendentals=0)


def params(mib):
    return pltpu.CompilerParams(vmem_limit_bytes=mib * MIB)


OWN_B, OWN_T, OTH_B, OTH_T, COUNT, LISTS = 0, 40, 80, 120, 160, 224


def make_lists(tile_ref, count_ref, lists):
    me = lax.axis_index(AXES)

    def step(b, counts):
        own_n, oth_n = counts
        tile = tile_ref[b]
        own = (lax.shift_right_logical(tile, 8) == me).astype(jnp.int32)
        lists[OWN_B + own_n] = b
        lists[OWN_T + own_n] = tile
        lists[OTH_B + oth_n] = b
        lists[OTH_T + oth_n] = tile
        lists[COUNT + b] = count_ref[b]
        return own_n + own, oth_n + 1 - own

    lax.fori_loop(0, BLK, step, (jnp.int32(0), jnp.int32(0)), unroll=4)


def cell_matrix(b, lists, index, weight):
    lanes = lax.broadcasted_iota(jnp.int32, (4, BLOCK), 1)
    points = lax.broadcasted_iota(jnp.int32, (BLOCK, BLOCK), 0).astype(F32).astype(BF16)
    zero = jnp.bfloat16(0)
    idx = index[b].astype(F32).astype(BF16)
    wgt = jnp.where(lanes < lists[COUNT + b], weight[b], 0.0).astype(BF16)
    mat = jnp.where(points == idx[0:1], wgt[0:1], zero)
    for k in range(1, 4):
        mat = mat + jnp.where(points == idx[k : k + 1], wgt[k : k + 1], zero)
    return mat


def spread_block(heights, mat):
    hi = heights.astype(BF16)
    lo = (heights - hi.astype(F32)).astype(BF16)
    both = lax.dot_general(
        jnp.concatenate([hi, lo], axis=0),
        mat,
        (((1,), (1,)), ((), ())),
        preferred_element_type=F32,
    )
    return both[:NF] + both[NF:]


def other_kernel(
    tile_hbm, count_hbm, ssh_hbm, index_hbm, weight_hbm, lists, wt_out, out,
    tile_ref, count_ref, ssh, index, weight, sems
):
    step = pl.program_id(0)

    @pl.when(step == 0)
    def _():
        pairs = [
            (tile_hbm, tile_ref),
            (count_hbm, count_ref),
            (index_hbm, index),
            (weight_hbm, weight),
            (ssh_hbm, ssh),
        ]
        copies = [pltpu.make_async_copy(s, d, sems.at[i]) for i, (s, d) in enumerate(pairs)]
        for copy in copies:
            copy.start()
        copies[0].wait()
        copies[1].wait()
        make_lists(tile_ref, count_ref, lists)
        me = lax.axis_index(AXES)
        lane = lax.broadcasted_iota(jnp.int32, (NF, BLOCK), 1)
        row = lax.broadcasted_iota(jnp.int32, (NF, BLOCK), 0)
        codes = jnp.zeros((NF, BLOCK), jnp.int32)
        for i in range(HALF_BLK):
            tile = lists[OTH_T + i]
            code = jnp.where(row == 0, tile & 255, lax.shift_right_logical(tile, 8) - me)
            codes = jnp.where((lane == i) & (row < 2), code, codes)
        out[HALF_BLK] = codes.astype(F32).astype(BF16)
        for copy in copies[2:]:
            copy.wait()

    for i in range(STEP):
        b = lists[OTH_B + step * STEP + i]
        mat = cell_matrix(b, lists, index, weight)
        wt_out[i] = mat
        out[step * STEP + i] = spread_block(ssh[b], mat).astype(BF16)


def spread_other(block_tile, cell_count, ssh, index, weight):
    return pl.pallas_call(
        other_kernel,
        grid=(HALF_BLK // STEP,),
        out_shape=(
            jax.ShapeDtypeStruct((LISTS,), jnp.int32),
            jax.ShapeDtypeStruct((HALF_BLK, BLOCK, BLOCK), BF16),
            jax.ShapeDtypeStruct((HALF_BLK + 1, NF, BLOCK), BF16),
        ),
        in_specs=[pl.BlockSpec(memory_space=pltpu.HBM)] * 5,
        out_specs=(
            smem_spec(),
            pl.BlockSpec((STEP, BLOCK, BLOCK), lambda i: (i, 0, 0)),
            pl.BlockSpec((HALF_BLK + 1, NF, BLOCK), lambda i: (0, 0, 0)),
        ),
        scratch_shapes=[
            SMEM((BLK,), jnp.int32),
            SMEM((BLK,), jnp.int32),
            VMEM((BLK, NF, BLOCK), F32),
            VMEM((BLK, 4, BLOCK), jnp.int32),
            VMEM((BLK, 4, BLOCK), F32),
            pltpu.SemaphoreType.DMA((5,)),
        ],
        compiler_params=params(60),
        cost_estimate=cost(5),
    )(block_tile, cell_count, ssh, index, weight)


def own_kernel(lists, ssh, index, weight, wt_out, grid):
    flip = jnp.where(lax.axis_index(AXES) >= DEVS // 2, 0xF0, 0)
    grid[...] = jnp.zeros_like(grid)

    def step(j, carry):
        for i in range(STEP):
            slot = j * STEP + i
            b = lists[OWN_B + slot]
            mat = cell_matrix(b, lists, index, weight)
            wt_out[slot] = mat
            tile = (lists[OWN_T + slot] & 255) ^ flip
            grid[tile] = grid[tile] + spread_block(ssh[b], mat)
        return carry

    lax.fori_loop(0, HALF_BLK // STEP, step, 0)


def spread_own(lists, ssh, index, weight):
    return pl.pallas_call(
        own_kernel,
        out_shape=(
            jax.ShapeDtypeStruct((HALF_BLK, BLOCK, BLOCK), BF16),
            jax.ShapeDtypeStruct((TILES + 1, NF, BLOCK), F32),
        ),
        in_specs=[smem_spec()] + [plain_spec()] * 3,
        out_specs=(vmem_spec(),) * 2,
        compiler_params=params(8),
        cost_estimate=cost(5),
    )(lists, ssh, index, weight)


def forward_kernel(
    start_grid, far, near, second, twc, tws, out, spots, grid, mid, wide, codes, sem
):
    del start_grid
    me = lax.axis_index(AXES)
    flip = jnp.where(me >= DEVS // 2, 0xF0, 0)
    rows = []
    from_below = jnp.where((me & 1) == 0, 1, -1)
    for values, direction in ((far, from_below), (near, -from_below)):
        code = values[HALF_BLK].astype(F32).astype(jnp.int32)
        rows.append(jnp.where(code[1:2] == direction, code[0:1] ^ flip, TILES))
    codes[0:2] = jnp.concatenate(rows, axis=0)[:, 0:128]
    copy = pltpu.make_async_copy(codes, spots, sem)
    copy.start()
    copy.wait()

    def add_other(i, carry):
        for side, values in enumerate((far, near)):
            spot = spots[side, i]
            grid[spot] = grid[spot] + values[i].astype(F32)
        return carry

    lax.fori_loop(0, HALF_BLK, add_other, 0, unroll=4)

    def circle(r, carry):
        for h in range(2):
            lanes = slice(h * 128, h * 128 + 128)
            re, im = real_dft16([grid[r * RADIX + s, :, lanes] for s in range(RADIX)])
            for u in range(RADIX):
                v = min(u, RADIX - u)
                cu, su = twc[u : u + 1, lanes], tws[u : u + 1, lanes]
                if u == 0:
                    x, y = re[0], jnp.zeros_like(re[0])
                elif u == 8:
                    x, y = re[8] * cu, -(re[8] * su)
                elif u < 8:
                    x, y = re[v] * cu + im[v] * su, im[v] * cu - re[v] * su
                else:
                    x, y = re[v] * cu - im[v] * su, -(im[v] * cu + re[v] * su)
                rows = slice(u * NF, u * NF + NF)
                mid[r, rows, h * 128 : h * 128 + 128] = x.astype(BF16)
                mid[r, rows, 256 + h * 128 : 256 + h * 128 + 128] = y.astype(BF16)
        return carry

    lax.fori_loop(0, LAT, circle, 0, unroll=2)
    for r in range(LAT):
        res = lax.dot_general(
            second[...], mid[r], (((1,), (1,)), ((), ())), preferred_element_type=F32
        )
        res = (res[:128] + res[128:]) * (1.0 / 4096.0)
        for c in range(2):
            for uh in range(2):
                wide[pl.ds(uh * 32 + c * 16 + r, NQ, stride=64), :] = res[
                    c * NQ : c * NQ + NQ, uh * 128 : uh * 128 + 128
                ]
    out[...] = wide[...].astype(BF16).reshape(out.shape)


def forward(grid, far, near, tables):
    fourier, spots, _ = pl.pallas_call(
        forward_kernel,
        out_shape=(
            jax.ShapeDtypeStruct((DEVS, 32, 128), BF16),
            jax.ShapeDtypeStruct((8, 128), jnp.int32),
            jax.ShapeDtypeStruct((TILES + 1, NF, BLOCK), F32),
        ),
        in_specs=[vmem_spec()] * 3 + [plain_spec()] * 3,
        out_specs=(vmem_spec(), smem_spec(), vmem_spec()),
        scratch_shapes=[
            VMEM((LAT, RADIX * NF, 2 * BLOCK), BF16),
            VMEM((DEVS * 32, 128), F32),
            VMEM((8, 128), jnp.int32),
            pltpu.SemaphoreType.DMA,
        ],
        input_output_aliases={0: 2},
        compiler_params=params(14),
        cost_estimate=cost(8),
    )(grid, far, near, tables["second"], tables["twc"], tables["tws"])
    return fourier, spots


def legendre_kernel(table, data, gauss, love, out, ins, outs):
    first_order = lax.axis_index(AXES) * ORD
    gw = gauss[...]
    for c in range(2):
        north = jnp.concatenate([data[i, c * 16 : c * 16 + 16] for i in range(64)], axis=0)
        south = jnp.concatenate([data[127 - i, c * 16 : c * 16 + 16] for i in range(64)], axis=0)
        north = north.astype(F32).T
        south = south.astype(F32).T
        even = ((north + south) * gw).astype(BF16)
        odd = ((north - south) * gw).astype(BF16)
        ins[:, c * 16 : c * 16 + 16, :] = even.reshape(ORD, NF, NLAT)
        ins[:, 32 + c * 16 : 32 + c * 16 + 16, :] = odd.reshape(ORD, NF, NLAT)
    degree = lax.broadcasted_iota(jnp.int32, (32, NDEG), 1)
    for k in range(ORD):
        both = jnp.dot(ins[k], table[k], preferred_element_type=F32)
        order = first_order + k
        is_even = ((degree + order) & 1) == 0
        coef = jnp.where(is_even, both[:32], both[32:])
        coef = jnp.where(degree < order, 0.0, coef)
        coef = coef * love[...]
        parts = jnp.concatenate(
            [jnp.where(is_even, coef, 0.0), jnp.where(is_even, 0.0, coef)], axis=0
        ).astype(BF16)
        res = lax.dot_general(
            parts, table[k], (((1,), (1,)), ((), ())), preferred_element_type=F32
        )
        upper = res[:32] + res[32:]
        lower = res[:32] - res[32:]
        for c in range(2):
            outs[c, 0, k * NF : k * NF + NF, :] = upper[c * 16 : c * 16 + 16]
            outs[c, 1, k * NF : k * NF + NF, :] = lower[c * 16 : c * 16 + 16]
    for c in range(2):
        up = outs[c, 0].T.astype(BF16)
        dn = outs[c, 1].T.astype(BF16)
        for i in range(64):
            out[i, c * 16 : c * 16 + 16] = up[i * 16 : i * 16 + 16]
            out[127 - i, c * 16 : c * 16 + 16] = dn[i * 16 : i * 16 + 16]


def legendre_both(table, data, gauss, love):
    return pl.pallas_call(
        legendre_kernel,
        out_shape=jax.ShapeDtypeStruct((DEVS, 32, 128), BF16),
        in_specs=[plain_spec(), vmem_spec(), plain_spec(), plain_spec()],
        out_specs=vmem_spec(),
        scratch_shapes=[VMEM((ORD, 64, NLAT), BF16), VMEM((2, 2, 128, NLAT), F32)],
        compiler_params=params(12),
        cost_estimate=cost(11),
    )(table, data, gauss.reshape(1, NLAT), love.reshape(1, NDEG))


def inverse_kernel(
    lists, spots, data, second, twc, tws, own, far, near, wide, tiles, waves
):
    me = lax.axis_index(AXES)
    flip = jnp.where(me >= DEVS // 2, 0xF0, 0)
    wide[...] = data[...].astype(F32).reshape(wide.shape)
    row = lax.broadcasted_iota(jnp.int32, (NQ, 128), 0)
    lane = lax.broadcasted_iota(jnp.int32, (NQ, 128), 1)
    zonal = jnp.where((row == 0) & (lane < NF), 1.0, 2.0)
    for r in range(LAT):
        parts = []
        for c in range(2):
            left = wide[pl.ds(c * 16 + r, NQ, stride=64), :] * zonal
            right = wide[pl.ds(32 + c * 16 + r, NQ, stride=64), :] * 2.0
            parts.append(jnp.concatenate([left, right], axis=1))
        spectrum = jnp.concatenate(parts, axis=0).T.astype(BF16)
        spectrum = jnp.concatenate([spectrum, spectrum], axis=1)
        waves[r] = jnp.dot(spectrum, second[...], preferred_element_type=F32)

    def circle(r, carry):
        for h in range(2):
            lanes = slice(h * 128, h * 128 + 128)
            re, im = {}, {}
            for u in range(RADIX):
                rows = slice(u * NF, u * NF + NF)
                x = waves[r, rows, h * 128 : h * 128 + 128]
                y = waves[r, rows, 256 + h * 128 : 256 + h * 128 + 128]
                cu, su = twc[u : u + 1, lanes], tws[u : u + 1, lanes]
                re[u] = x * cu - y * su if u else x
                if u not in (0, 8):
                    im[u] = x * su + y * cu
            a = [re[0]] + [re[u] + re[RADIX - u] for u in range(1, 8)] + [re[8]]
            b = [None] + [im[u] - im[RADIX - u] for u in range(1, 8)]
            values = real_idft16(a, b)
            for s in range(RADIX):
                tiles[r * RADIX + s, :, lanes] = values[s]
        return carry

    lax.fori_loop(0, LAT, circle, 0)

    def gather(i, carry):
        own[i] = tiles[(lists[OWN_T + i] & 255) ^ flip]
        far[i] = tiles[spots[0, i] & 255].astype(BF16)
        near[i] = tiles[spots[1, i] & 255].astype(BF16)
        return carry

    lax.fori_loop(0, HALF_BLK, gather, 0, unroll=4)


def inverse(lists, spots, data, tables):
    return pl.pallas_call(
        inverse_kernel,
        out_shape=(
            jax.ShapeDtypeStruct((HALF_BLK, NF, BLOCK), F32),
            jax.ShapeDtypeStruct((HALF_BLK, NF, BLOCK), BF16),
            jax.ShapeDtypeStruct((HALF_BLK, NF, BLOCK), BF16),
        ),
        in_specs=[smem_spec()] * 2 + [vmem_spec()] + [plain_spec()] * 3,
        out_specs=(vmem_spec(),) * 3,
        scratch_shapes=[
            VMEM((DEVS * 32, 128), F32),
            VMEM((TILES, NF, BLOCK), F32),
            VMEM((LAT, RADIX * NF, 2 * BLOCK), F32),
        ],
        compiler_params=params(20),
        cost_estimate=cost(7),
    )(lists, spots, data, tables["second"], tables["twc"], tables["tws"])


def own_cells_kernel(values, wt, out):
    for i in range(HALF_BLK):
        val = values[i]
        hi = val.astype(BF16)
        lo = (val - hi.astype(F32)).astype(BF16)
        both = jnp.dot(jnp.concatenate([hi, lo], axis=0), wt[i], preferred_element_type=F32)
        out[i] = both[:NF] + both[NF:]


def own_cells(values, wt):
    return pl.pallas_call(
        own_cells_kernel,
        out_shape=jax.ShapeDtypeStruct((HALF_BLK, NF, BLOCK), F32),
        in_specs=[vmem_spec()] * 2,
        out_specs=vmem_spec(),
        compiler_params=params(6),
        cost_estimate=cost(2),
    )(values, wt)


def cells_kernel(lists, own, far, near, wt, out, res, sems):
    me = lax.axis_index(AXES)
    odd = (me & 1) == 1
    own_copies = [
        pltpu.make_async_copy(own.at[i], out.at[lists[OWN_B + i]], sems.at[i])
        for i in range(HALF_BLK)
    ]
    for copy in own_copies:
        copy.start()
    copies = []
    for i in range(HALF_BLK):
        above = lax.shift_right_logical(lists[OTH_T + i], 8) > me
        val = jnp.where(above == odd, far[i], near[i])
        res[i] = jnp.dot(val, wt[i], preferred_element_type=F32)
        copy = pltpu.make_async_copy(
            res.at[i], out.at[lists[OTH_B + i]], sems.at[HALF_BLK + i]
        )
        copy.start()
        copies.append(copy)
    for copy in own_copies + copies:
        copy.wait()


def all_cells(lists, own, far, near, wt):
    return pl.pallas_call(
        cells_kernel,
        out_shape=jax.ShapeDtypeStruct((BLK, NF, BLOCK), F32),
        in_specs=[smem_spec()] + [vmem_spec()] * 3 + [plain_spec()],
        out_specs=pl.BlockSpec(memory_space=pltpu.HBM),
        scratch_shapes=[VMEM((HALF_BLK, NF, BLOCK), F32), pltpu.SemaphoreType.DMA((BLK,))],
        compiler_params=params(8),
        cost_estimate=cost(4),
    )(lists, own, far, near, wt)


def swap(value, first):
    pairs = []
    for i in range(first, DEVS - 1, 2):
        pairs += [(i, i + 1), (i + 1, i)]
    return lax.ppermute(value, AXES, pairs)


def on_device(
    tables, ssh, cell_count, remap_index, remap_weight, block_tile, gauss_weight, love, legendre
):
    lists, wt_oth, oth = spread_other(block_tile, cell_count, ssh, remap_index, remap_weight)
    far = swap(oth, 1)
    near = swap(oth, 0)
    wt_own, grid = spread_own(lists, ssh, remap_index, remap_weight)
    fourier, spots = forward(grid, far, near, tables)
    by_order = lax.all_to_all(fourier, AXES, split_axis=0, concat_axis=0, tiled=True)
    synth = legendre_both(legendre, by_order, gauss_weight, love)
    by_lat = lax.all_to_all(synth, AXES, split_axis=0, concat_axis=0, tiled=True)
    own_v, far_v, near_v = inverse(lists, spots, by_lat, tables)
    from_far = swap(far_v, 1)
    from_near = swap(near_v, 0)
    own_cell = own_cells(own_v, wt_own)
    return all_cells(lists, own_cell, from_far, from_near, wt_oth)


def solution(mesh):
    tables = {name: jnp.asarray(table) for name, table in make_tables().items()}
    return jax.shard_map(
        functools.partial(on_device, tables),
        mesh=mesh,
        in_specs=(
            P(AXES, None, None),
            P(AXES),
            P(AXES, None, None),
            P(AXES, None, None),
            P(AXES),
            P(),
            P(),
            P(AXES, None, None),
        ),
        out_specs=P(AXES, None, None),
        check_vma=False,
    )
```

```python
import functools
import math

import jax
import jax.numpy as jnp
import numpy as np
from jax import lax
from jax.experimental import pallas as pl
from jax.experimental.pallas import tpu as pltpu
from jax.sharding import PartitionSpec as P

AXES = ("dom", "order")
DEVS = 128
NF = 16
BLOCK = 256
BLK = 64
HALF_BLK = 32
TILES = 256
LAT = 16
ORD = 8
NLAT = 1024
NDEG = 1024
RADIX = 16
NQ = 64
STEP = 8
F32 = jnp.float32
BF16 = jnp.bfloat16
MIB = 1 << 20

SMEM = pltpu.SMEM
VMEM = pltpu.VMEM


def hi_lo(table):
    table = np.asarray(table, np.float32)
    hi = table.astype(jnp.bfloat16)
    lo = (table - hi.astype(np.float32)).astype(jnp.bfloat16)
    return hi, lo


def make_tables():
    points = np.arange(BLOCK)
    angle = 2 * np.pi * ((np.arange(NQ)[:, None] * points[None, :]) % BLOCK) / BLOCK
    cos, sin = np.cos(angle), np.sin(angle)
    second = np.concatenate(
        [np.concatenate([cos, sin], axis=1), np.concatenate([-sin, cos], axis=1)], axis=0
    )
    s_hi, s_lo = hi_lo(second)
    twist = 2 * np.pi * (np.arange(RADIX)[:, None] * points[None, :]) / 4096.0
    return dict(
        second=np.concatenate([s_hi, s_lo], axis=0),
        twc=np.cos(twist).astype(np.float32),
        tws=np.sin(twist).astype(np.float32),
    )


ROOT = math.sqrt(0.5)
COS1 = math.cos(math.pi / 8)
SIN1 = math.sin(math.pi / 8)


def real_dft16(g):
    e = [g[s] + g[s + 8] for s in range(8)]
    o = [g[s] - g[s + 8] for s in range(8)]
    re, im = [None] * 9, [None] * 9
    ee = [e[s] + e[s + 4] for s in range(4)]
    eo = [e[s] - e[s + 4] for s in range(4)]
    x, y = ee[0] + ee[2], ee[1] + ee[3]
    re[0], re[8] = x + y, x - y
    re[4], im[4] = ee[0] - ee[2], ee[3] - ee[1]

    def odd4(p):
        d, s = (p[1] - p[3]) * ROOT, (p[1] + p[3]) * ROOT
        return (p[0] + d, -(s + p[2])), (p[0] - d, p[2] - s)

    (re[2], im[2]), (re[6], im[6]) = odd4(eo)
    a1, a3 = odd4(o[0::2])
    b1, b3 = odd4(o[1::2])
    t = (b1[0] * COS1 + b1[1] * SIN1, b1[1] * COS1 - b1[0] * SIN1)
    re[1], im[1] = a1[0] + t[0], a1[1] + t[1]
    re[7], im[7] = a1[0] - t[0], t[1] - a1[1]
    t = (b3[0] * SIN1 + b3[1] * COS1, b3[1] * SIN1 - b3[0] * COS1)
    re[3], im[3] = a3[0] + t[0], a3[1] + t[1]
    re[5], im[5] = a3[0] - t[0], t[1] - a3[1]
    return re, im


def real_idft16(a, b):
    x, z = a[0] + a[8], a[0] - a[8]
    q = [x + a[4], z - b[4], x - a[4], z + b[4]]

    def odd4(p1, p3):
        d, s = (p1[0] - p3[0]) * ROOT, (p1[1] + p3[1]) * ROOT
        return [p1[0] + p3[0], d - s, p3[1] - p1[1], -(d + s)]

    w = odd4((a[2], b[2]), (a[6], b[6]))
    even = [q[t] + w[t] for t in range(4)] + [q[t] - w[t] for t in range(4)]
    p1, q1 = (a[1] + a[7], b[1] - b[7]), (a[1] - a[7], b[1] + b[7])
    p3, q3 = (a[3] + a[5], b[3] - b[5]), (a[3] - a[5], b[3] + b[5])
    q1 = (q1[0] * COS1 - q1[1] * SIN1, q1[0] * SIN1 + q1[1] * COS1)
    q3 = (q3[0] * SIN1 - q3[1] * COS1, q3[0] * COS1 + q3[1] * SIN1)
    oe, oo = odd4(p1, p3), odd4(q1, q3)
    odd = [oe[s // 2] if s % 2 == 0 else oo[s // 2] for s in range(8)]
    return [even[s] + odd[s] for s in range(8)] + [even[s] - odd[s] for s in range(8)]


def vmem_spec():
    return pl.BlockSpec(memory_space=VMEM)


def smem_spec():
    return pl.BlockSpec(memory_space=SMEM)


def plain_spec():
    return pl.BlockSpec()


def cost(micros):
    return pl.CostEstimate(flops=micros * 10**9, bytes_accessed=4 * MIB, transcendentals=0)


def params(mib):
    return pltpu.CompilerParams(vmem_limit_bytes=mib * MIB)


OWN_B, OWN_T, OTH_B, OTH_T, COUNT, LISTS = 0, 40, 80, 120, 160, 224


def make_lists(tile_ref, count_ref, lists):
    me = lax.axis_index(AXES)

    def step(b, counts):
        own_n, oth_n = counts
        tile = tile_ref[b]
        own = (lax.shift_right_logical(tile, 8) == me).astype(jnp.int32)
        lists[OWN_B + own_n] = b
        lists[OWN_T + own_n] = tile
        lists[OTH_B + oth_n] = b
        lists[OTH_T + oth_n] = tile
        lists[COUNT + b] = count_ref[b]
        return own_n + own, oth_n + 1 - own

    lax.fori_loop(0, BLK, step, (jnp.int32(0), jnp.int32(0)), unroll=4)


def cell_matrix(b, lists, index, weight):
    lanes = lax.broadcasted_iota(jnp.int32, (4, BLOCK), 1)
    points = lax.broadcasted_iota(jnp.int32, (BLOCK, BLOCK), 0).astype(F32).astype(BF16)
    raw = index[b]
    wgt = jnp.where(lanes < lists[COUNT + b], weight[b], 0.0)
    sums = []
    for k in range(4):
        total = wgt[k : k + 1]
        for j in range(k + 1, 4):
            same = raw[j : j + 1] == raw[k : k + 1]
            total = total + jnp.where(same, wgt[j : j + 1], 0.0)
        sums.append(total.astype(BF16))
    idx = raw.astype(F32).astype(BF16)
    mat = jnp.where(points == idx[3:4], sums[3], jnp.bfloat16(0))
    for k in (2, 1, 0):
        mat = jnp.where(points == idx[k : k + 1], sums[k], mat)
    return mat


def spread_block(heights, mat):
    hi = heights.astype(BF16)
    lo = (heights - hi.astype(F32)).astype(BF16)
    both = lax.dot_general(
        jnp.concatenate([hi, lo], axis=0),
        mat,
        (((1,), (1,)), ((), ())),
        preferred_element_type=F32,
    )
    return both[:NF] + both[NF:]


def other_kernel(
    tile_hbm, count_hbm, ssh_hbm, index_hbm, weight_hbm, lists, wt_out, out,
    tile_ref, count_ref, ssh, index, weight, sems
):
    step = pl.program_id(0)

    @pl.when(step == 0)
    def _():
        pairs = [
            (tile_hbm, tile_ref),
            (count_hbm, count_ref),
            (index_hbm, index),
            (weight_hbm, weight),
            (ssh_hbm, ssh),
        ]
        copies = [pltpu.make_async_copy(s, d, sems.at[i]) for i, (s, d) in enumerate(pairs)]
        for copy in copies:
            copy.start()
        copies[0].wait()
        copies[1].wait()
        make_lists(tile_ref, count_ref, lists)
        me = lax.axis_index(AXES)
        lane = lax.broadcasted_iota(jnp.int32, (NF, BLOCK), 1)
        row = lax.broadcasted_iota(jnp.int32, (NF, BLOCK), 0)
        codes = jnp.zeros((NF, BLOCK), jnp.int32)
        for i in range(HALF_BLK):
            tile = lists[OTH_T + i]
            code = jnp.where(row == 0, tile & 255, lax.shift_right_logical(tile, 8) - me)
            codes = jnp.where((lane == i) & (row < 2), code, codes)
        out[HALF_BLK] = codes.astype(F32).astype(BF16)
        for copy in copies[2:]:
            copy.wait()

    for i in range(STEP):
        b = lists[OTH_B + step * STEP + i]
        mat = cell_matrix(b, lists, index, weight)
        wt_out[i] = mat
        out[step * STEP + i] = spread_block(ssh[b], mat).astype(BF16)


def copy_kernel(source, out):
    out[...] = source[...]


def later_copy(value):
    return pl.pallas_call(
        copy_kernel,
        out_shape=jax.ShapeDtypeStruct(value.shape, value.dtype),
        in_specs=[vmem_spec()],
        out_specs=vmem_spec(),
        compiler_params=params(2),
        cost_estimate=cost(3),
    )(value)


def spread_other(block_tile, cell_count, ssh, index, weight):
    return pl.pallas_call(
        other_kernel,
        grid=(HALF_BLK // STEP,),
        out_shape=(
            jax.ShapeDtypeStruct((LISTS,), jnp.int32),
            jax.ShapeDtypeStruct((HALF_BLK, BLOCK, BLOCK), BF16),
            jax.ShapeDtypeStruct((HALF_BLK + 1, NF, BLOCK), BF16),
        ),
        in_specs=[pl.BlockSpec(memory_space=pltpu.HBM)] * 5,
        out_specs=(
            smem_spec(),
            pl.BlockSpec((STEP, BLOCK, BLOCK), lambda i: (i, 0, 0)),
            pl.BlockSpec((HALF_BLK + 1, NF, BLOCK), lambda i: (0, 0, 0)),
        ),
        scratch_shapes=[
            SMEM((BLK,), jnp.int32),
            SMEM((BLK,), jnp.int32),
            VMEM((BLK, NF, BLOCK), F32),
            VMEM((BLK, 4, BLOCK), jnp.int32),
            VMEM((BLK, 4, BLOCK), F32),
            pltpu.SemaphoreType.DMA((5,)),
        ],
        compiler_params=params(60),
        cost_estimate=cost(5),
    )(block_tile, cell_count, ssh, index, weight)


def own_kernel(lists, ssh, index, weight, wt_out, grid):
    flip = jnp.where(lax.axis_index(AXES) >= DEVS // 2, 0xF0, 0)
    grid[...] = jnp.zeros_like(grid)

    def step(j, carry):
        for i in range(STEP):
            slot = j * STEP + i
            b = lists[OWN_B + slot]
            mat = cell_matrix(b, lists, index, weight)
            wt_out[slot] = mat
            tile = (lists[OWN_T + slot] & 255) ^ flip
            grid[tile] = grid[tile] + spread_block(ssh[b], mat)
        return carry

    lax.fori_loop(0, HALF_BLK // STEP, step, 0)


def spread_own(lists, ssh, index, weight):
    return pl.pallas_call(
        own_kernel,
        out_shape=(
            jax.ShapeDtypeStruct((HALF_BLK, BLOCK, BLOCK), BF16),
            jax.ShapeDtypeStruct((TILES + 1, NF, BLOCK), F32),
        ),
        in_specs=[smem_spec()] + [plain_spec()] * 3,
        out_specs=(vmem_spec(),) * 2,
        compiler_params=params(8),
        cost_estimate=cost(5),
    )(lists, ssh, index, weight)


def forward_kernel(
    start_grid, far, near, second, twc, tws, out, spots, grid, mid, wide, codes, sem
):
    del start_grid
    me = lax.axis_index(AXES)
    flip = jnp.where(me >= DEVS // 2, 0xF0, 0)
    rows = []
    from_below = jnp.where((me & 1) == 0, 1, -1)
    for values, direction in ((far, from_below), (near, -from_below)):
        code = values[HALF_BLK].astype(F32).astype(jnp.int32)
        rows.append(jnp.where(code[1:2] == direction, code[0:1] ^ flip, TILES))
    codes[0:2] = jnp.concatenate(rows, axis=0)[:, 0:128]
    copy = pltpu.make_async_copy(codes, spots, sem)
    copy.start()
    copy.wait()

    def add_other(i, carry):
        for side, values in enumerate((far, near)):
            spot = spots[side, i]
            grid[spot] = grid[spot] + values[i].astype(F32)
        return carry

    lax.fori_loop(0, HALF_BLK, add_other, 0, unroll=4)

    def circle(r):
        for h in range(2):
            lanes = slice(h * 128, h * 128 + 128)
            re, im = real_dft16([grid[r * RADIX + s, :, lanes] for s in range(RADIX)])
            for u in range(RADIX):
                v = min(u, RADIX - u)
                cu, su = twc[u : u + 1, lanes], tws[u : u + 1, lanes]
                if u == 0:
                    x, y = re[0], jnp.zeros_like(re[0])
                elif u == 8:
                    x, y = re[8] * cu, -(re[8] * su)
                elif u < 8:
                    x, y = re[v] * cu + im[v] * su, im[v] * cu - re[v] * su
                else:
                    x, y = re[v] * cu - im[v] * su, -(im[v] * cu + re[v] * su)
                rows = slice(u * NF, u * NF + NF)
                mid[r, rows, h * 128 : h * 128 + 128] = x.astype(BF16)
                mid[r, rows, 256 + h * 128 : 256 + h * 128 + 128] = y.astype(BF16)

    def waves(r):
        res = lax.dot_general(
            second[...], mid[r], (((1,), (1,)), ((), ())), preferred_element_type=F32
        )
        res = (res[:128] + res[128:]) * (1.0 / 4096.0)
        for c in range(2):
            for uh in range(2):
                wide[pl.ds(uh * 32 + c * 16 + r, NQ, stride=64), :] = res[
                    c * NQ : c * NQ + NQ, uh * 128 : uh * 128 + 128
                ]

    circle(0)
    for r in range(1, LAT):
        waves(r - 1)
        circle(r)
    waves(LAT - 1)
    out[...] = wide[...].astype(BF16).reshape(out.shape)


def forward(grid, far, near, tables):
    fourier, spots, _ = pl.pallas_call(
        forward_kernel,
        out_shape=(
            jax.ShapeDtypeStruct((DEVS, 32, 128), BF16),
            jax.ShapeDtypeStruct((8, 128), jnp.int32),
            jax.ShapeDtypeStruct((TILES + 1, NF, BLOCK), F32),
        ),
        in_specs=[vmem_spec()] * 3 + [plain_spec()] * 3,
        out_specs=(vmem_spec(), smem_spec(), vmem_spec()),
        scratch_shapes=[
            VMEM((LAT, RADIX * NF, 2 * BLOCK), BF16),
            VMEM((DEVS * 32, 128), F32),
            VMEM((8, 128), jnp.int32),
            pltpu.SemaphoreType.DMA,
        ],
        input_output_aliases={0: 2},
        compiler_params=params(14),
        cost_estimate=cost(8),
    )(grid, far, near, tables["second"], tables["twc"], tables["tws"])
    return fourier, spots


def legendre_kernel(table, data, gauss, love, out, ins, coefs):
    first_order = lax.axis_index(AXES) * ORD
    gw = gauss[...]
    for c in range(2):
        north = jnp.concatenate([data[i, c * 16 : c * 16 + 16] for i in range(64)], axis=0)
        south = jnp.concatenate([data[127 - i, c * 16 : c * 16 + 16] for i in range(64)], axis=0)
        north = north.astype(F32).T
        south = south.astype(F32).T
        even = ((north + south) * gw).astype(BF16)
        odd = ((north - south) * gw).astype(BF16)
        ins[:, c * 16 : c * 16 + 16, :] = even.reshape(ORD, NF, NLAT)
        ins[:, 32 + c * 16 : 32 + c * 16 + 16, :] = odd.reshape(ORD, NF, NLAT)
    degree = lax.broadcasted_iota(jnp.int32, (32, NDEG), 1)
    lane_order = lax.shift_right_logical(lax.broadcasted_iota(jnp.int32, (NLAT, 256), 1), 4) & 3
    for high in range(2):
        for low in range(4):
            k = high * 4 + low
            both = jnp.dot(ins[k], table[k], preferred_element_type=F32)
            order = first_order + k
            is_even = ((degree + order) & 1) == 0
            coef = jnp.where(is_even, both[:32], both[32:])
            coef = jnp.where(degree < order, 0.0, coef)
            coef = coef * love[...]
            mirror = jnp.where(is_even, coef, -coef)
            for side, values in enumerate((coef, mirror)):
                for c in range(2):
                    spot = side * 128 + c * 64 + low * NF
                    coefs[high, spot : spot + NF, :] = values[c * NF : c * NF + NF].astype(BF16)
        columns = coefs[high].T
        total = jnp.zeros((NLAT, 256), F32)
        for low in range(4):
            res = jnp.dot(table[high * 4 + low], columns, preferred_element_type=F32)
            total = jnp.where(lane_order == low, res, total)
        total = total.astype(BF16)
        for i in range(64):
            rows = slice(i * 16, i * 16 + 16)
            out[i, high * 16 : high * 16 + 16] = total[rows, 0:128]
            out[127 - i, high * 16 : high * 16 + 16] = total[rows, 128:256]


def legendre_both(table, data, gauss, love):
    return pl.pallas_call(
        legendre_kernel,
        out_shape=jax.ShapeDtypeStruct((DEVS, 32, 128), BF16),
        in_specs=[plain_spec(), vmem_spec(), plain_spec(), plain_spec()],
        out_specs=vmem_spec(),
        scratch_shapes=[VMEM((ORD, 64, NLAT), BF16), VMEM((2, 256, NDEG), BF16)],
        compiler_params=params(12),
        cost_estimate=cost(11),
    )(table, data, gauss.reshape(1, NLAT), love.reshape(1, NDEG))


def inverse_kernel(
    lists, spots, data, second, twc, tws, own, far, near, wide, tiles, waves
):
    me = lax.axis_index(AXES)
    flip = jnp.where(me >= DEVS // 2, 0xF0, 0)
    wide[...] = data[...].astype(F32).reshape(wide.shape)
    row = lax.broadcasted_iota(jnp.int32, (NQ, 128), 0)
    lane = lax.broadcasted_iota(jnp.int32, (NQ, 128), 1)
    zonal = jnp.where((row == 0) & ((lane & 63) < NF), 1.0, 2.0)
    left = lane < 64

    def spread_waves(r):
        parts = [[], []]
        for uh in range(2):
            first = wide[pl.ds(uh * 32 + r, NQ, stride=64), :] * (2.0 if uh else zonal)
            second_half = wide[pl.ds(uh * 32 + 16 + r, NQ, stride=64), :] * 2.0
            parts[0].append(jnp.where(left, first, pltpu.roll(second_half, 64, 1)))
            parts[1].append(jnp.where(left, pltpu.roll(first, 64, 1), second_half))
        parts = [jnp.concatenate(part, axis=1) for part in parts]
        spectrum = jnp.concatenate(parts, axis=0).T.astype(BF16)
        spectrum = jnp.concatenate([spectrum, spectrum], axis=1)
        waves[r] = jnp.dot(spectrum, second[...], preferred_element_type=F32)

    def circle(r):
        for h in range(2):
            lanes = slice(h * 128, h * 128 + 128)
            re, im = {}, {}
            for u in range(RADIX):
                rows = slice(u * NF, u * NF + NF)
                x = waves[r, rows, h * 128 : h * 128 + 128]
                y = waves[r, rows, 256 + h * 128 : 256 + h * 128 + 128]
                cu, su = twc[u : u + 1, lanes], tws[u : u + 1, lanes]
                re[u] = x * cu - y * su if u else x
                if u not in (0, 8):
                    im[u] = x * su + y * cu
            a = [re[0]] + [re[u] + re[RADIX - u] for u in range(1, 8)] + [re[8]]
            b = [None] + [im[u] - im[RADIX - u] for u in range(1, 8)]
            values = real_idft16(a, b)
            for s in range(RADIX):
                tiles[r * RADIX + s, :, lanes] = values[s]

    spread_waves(0)
    for r in range(1, LAT):
        spread_waves(r)
        circle(r - 1)
    circle(LAT - 1)

    def gather(i, carry):
        own[i] = tiles[(lists[OWN_T + i] & 255) ^ flip]
        far[i] = tiles[spots[0, i] & 255].astype(BF16)
        near[i] = tiles[spots[1, i] & 255].astype(BF16)
        return carry

    lax.fori_loop(0, HALF_BLK, gather, 0, unroll=4)


def inverse(lists, spots, data, tables):
    return pl.pallas_call(
        inverse_kernel,
        out_shape=(
            jax.ShapeDtypeStruct((HALF_BLK, NF, BLOCK), F32),
            jax.ShapeDtypeStruct((HALF_BLK, NF, BLOCK), BF16),
            jax.ShapeDtypeStruct((HALF_BLK, NF, BLOCK), BF16),
        ),
        in_specs=[smem_spec()] * 2 + [vmem_spec()] + [plain_spec()] * 3,
        out_specs=(vmem_spec(),) * 3,
        scratch_shapes=[
            VMEM((DEVS * 32, 128), F32),
            VMEM((TILES, NF, BLOCK), F32),
            VMEM((LAT, RADIX * NF, 2 * BLOCK), F32),
        ],
        compiler_params=params(20),
        cost_estimate=cost(7),
    )(lists, spots, data, tables["second"], tables["twc"], tables["tws"])


def own_cells_kernel(lists, values, wt, out, res, sems):
    copies = []
    for i in range(HALF_BLK):
        val = values[i]
        hi = val.astype(BF16)
        lo = (val - hi.astype(F32)).astype(BF16)
        both = jnp.dot(jnp.concatenate([hi, lo], axis=0), wt[i], preferred_element_type=F32)
        res[i] = both[:NF] + both[NF:]
        copy = pltpu.make_async_copy(res.at[i], out.at[lists[OWN_B + i]], sems.at[i])
        copy.start()
        copies.append(copy)
    for copy in copies:
        copy.wait()


def own_cells(lists, values, wt):
    return pl.pallas_call(
        own_cells_kernel,
        out_shape=jax.ShapeDtypeStruct((BLK, NF, BLOCK), F32),
        in_specs=[smem_spec()] + [vmem_spec()] * 2,
        out_specs=pl.BlockSpec(memory_space=pltpu.HBM),
        scratch_shapes=[VMEM((HALF_BLK, NF, BLOCK), F32), pltpu.SemaphoreType.DMA((HALF_BLK,))],
        compiler_params=params(6),
        cost_estimate=cost(2),
    )(lists, values, wt)


def cells_kernel(lists, own, far, near, wt, out, res, sems):
    del own
    me = lax.axis_index(AXES)
    odd = (me & 1) == 1
    copies = []
    for i in range(HALF_BLK):
        above = lax.shift_right_logical(lists[OTH_T + i], 8) > me
        val = jnp.where(above == odd, far[i], near[i])
        res[i] = jnp.dot(val, wt[i], preferred_element_type=F32)
        copy = pltpu.make_async_copy(res.at[i], out.at[lists[OTH_B + i]], sems.at[i])
        copy.start()
        copies.append(copy)
    for copy in copies:
        copy.wait()


def all_cells(lists, own, far, near, wt):
    return pl.pallas_call(
        cells_kernel,
        out_shape=jax.ShapeDtypeStruct((BLK, NF, BLOCK), F32),
        in_specs=[smem_spec(), pl.BlockSpec(memory_space=pltpu.HBM)]
        + [vmem_spec()] * 2
        + [plain_spec()],
        out_specs=pl.BlockSpec(memory_space=pltpu.HBM),
        scratch_shapes=[VMEM((HALF_BLK, NF, BLOCK), F32), pltpu.SemaphoreType.DMA((HALF_BLK,))],
        input_output_aliases={1: 0},
        compiler_params=params(8),
        cost_estimate=cost(4),
    )(lists, own, far, near, wt)


def swap(value, first):
    pairs = []
    for i in range(first, DEVS - 1, 2):
        pairs += [(i, i + 1), (i + 1, i)]
    return lax.ppermute(value, AXES, pairs)


def on_device(
    tables, ssh, cell_count, remap_index, remap_weight, block_tile, gauss_weight, love, legendre
):
    lists, wt_oth, oth = spread_other(block_tile, cell_count, ssh, remap_index, remap_weight)
    far = swap(oth, 1)
    near = swap(later_copy(oth), 0)
    wt_own, grid = spread_own(lists, ssh, remap_index, remap_weight)
    fourier, spots = forward(grid, far, near, tables)
    by_order = lax.all_to_all(fourier, AXES, split_axis=0, concat_axis=0, tiled=True)
    synth = legendre_both(legendre, by_order, gauss_weight, love)
    by_lat = lax.all_to_all(synth, AXES, split_axis=0, concat_axis=0, tiled=True)
    own_v, far_v, near_v = inverse(lists, spots, by_lat, tables)
    from_far = swap(far_v, 1)
    from_near = swap(near_v, 0)
    own_cell = own_cells(lists, own_v, wt_own)
    return all_cells(lists, own_cell, from_far, from_near, wt_oth)


def solution(mesh):
    tables = {name: jnp.asarray(table) for name, table in make_tables().items()}
    return jax.shard_map(
        functools.partial(on_device, tables),
        mesh=mesh,
        in_specs=(
            P(AXES, None, None),
            P(AXES),
            P(AXES, None, None),
            P(AXES, None, None),
            P(AXES),
            P(),
            P(),
            P(AXES, None, None),
        ),
        out_specs=P(AXES, None, None),
        check_vma=False,
    )
```

```python
import functools
import math

import jax
import jax.numpy as jnp
import numpy as np
from jax import lax
from jax.experimental import pallas as pl
from jax.experimental.pallas import tpu as pltpu
from jax.sharding import PartitionSpec as P

AXES = ("dom", "order")
DEVS = 128
NF = 16
BLOCK = 256
BLK = 64
HALF_BLK = 32
TILES = 256
LAT = 16
ORD = 8
NLAT = 1024
NDEG = 1024
RADIX = 16
NQ = 64
STEP = 8
F32 = jnp.float32
BF16 = jnp.bfloat16
MIB = 1 << 20

SMEM = pltpu.SMEM
VMEM = pltpu.VMEM


def hi_lo(table):
    table = np.asarray(table, np.float32)
    hi = table.astype(jnp.bfloat16)
    lo = (table - hi.astype(np.float32)).astype(jnp.bfloat16)
    return hi, lo


def make_tables():
    points = np.arange(BLOCK)
    angle = 2 * np.pi * ((np.arange(NQ)[:, None] * points[None, :]) % BLOCK) / BLOCK
    cos, sin = np.cos(angle), np.sin(angle)
    second = np.concatenate(
        [np.concatenate([cos, sin], axis=1), np.concatenate([-sin, cos], axis=1)], axis=0
    )
    s_hi, s_lo = hi_lo(second)
    twist = 2 * np.pi * (np.arange(RADIX)[:, None] * points[None, :]) / 4096.0
    return dict(
        second=np.concatenate([s_hi, s_lo], axis=0),
        twc=np.cos(twist).astype(np.float32),
        tws=np.sin(twist).astype(np.float32),
    )


ROOT = math.sqrt(0.5)
COS1 = math.cos(math.pi / 8)
SIN1 = math.sin(math.pi / 8)


def real_dft16(g):
    e = [g[s] + g[s + 8] for s in range(8)]
    o = [g[s] - g[s + 8] for s in range(8)]
    re, im = [None] * 9, [None] * 9
    ee = [e[s] + e[s + 4] for s in range(4)]
    eo = [e[s] - e[s + 4] for s in range(4)]
    x, y = ee[0] + ee[2], ee[1] + ee[3]
    re[0], re[8] = x + y, x - y
    re[4], im[4] = ee[0] - ee[2], ee[3] - ee[1]

    def odd4(p):
        d, s = (p[1] - p[3]) * ROOT, (p[1] + p[3]) * ROOT
        return (p[0] + d, -(s + p[2])), (p[0] - d, p[2] - s)

    (re[2], im[2]), (re[6], im[6]) = odd4(eo)
    a1, a3 = odd4(o[0::2])
    b1, b3 = odd4(o[1::2])
    t = (b1[0] * COS1 + b1[1] * SIN1, b1[1] * COS1 - b1[0] * SIN1)
    re[1], im[1] = a1[0] + t[0], a1[1] + t[1]
    re[7], im[7] = a1[0] - t[0], t[1] - a1[1]
    t = (b3[0] * SIN1 + b3[1] * COS1, b3[1] * SIN1 - b3[0] * COS1)
    re[3], im[3] = a3[0] + t[0], a3[1] + t[1]
    re[5], im[5] = a3[0] - t[0], t[1] - a3[1]
    return re, im


def real_idft16(a, b):
    x, z = a[0] + a[8], a[0] - a[8]
    q = [x + a[4], z - b[4], x - a[4], z + b[4]]

    def odd4(p1, p3):
        d, s = (p1[0] - p3[0]) * ROOT, (p1[1] + p3[1]) * ROOT
        return [p1[0] + p3[0], d - s, p3[1] - p1[1], -(d + s)]

    w = odd4((a[2], b[2]), (a[6], b[6]))
    even = [q[t] + w[t] for t in range(4)] + [q[t] - w[t] for t in range(4)]
    p1, q1 = (a[1] + a[7], b[1] - b[7]), (a[1] - a[7], b[1] + b[7])
    p3, q3 = (a[3] + a[5], b[3] - b[5]), (a[3] - a[5], b[3] + b[5])
    q1 = (q1[0] * COS1 - q1[1] * SIN1, q1[0] * SIN1 + q1[1] * COS1)
    q3 = (q3[0] * SIN1 - q3[1] * COS1, q3[0] * COS1 + q3[1] * SIN1)
    oe, oo = odd4(p1, p3), odd4(q1, q3)
    odd = [oe[s // 2] if s % 2 == 0 else oo[s // 2] for s in range(8)]
    return [even[s] + odd[s] for s in range(8)] + [even[s] - odd[s] for s in range(8)]


def vmem_spec():
    return pl.BlockSpec(memory_space=VMEM)


def smem_spec():
    return pl.BlockSpec(memory_space=SMEM)


def plain_spec():
    return pl.BlockSpec()


def cost(micros):
    return pl.CostEstimate(flops=micros * 10**9, bytes_accessed=4 * MIB, transcendentals=0)


def params(mib):
    return pltpu.CompilerParams(vmem_limit_bytes=mib * MIB)


OWN_B, OWN_T, OTH_B, OTH_T, COUNT, LISTS = 0, 40, 80, 120, 160, 224


def make_lists(tile_ref, count_ref, lists):
    me = lax.axis_index(AXES)

    def step(b, counts):
        own_n, oth_n = counts
        tile = tile_ref[b]
        own = (lax.shift_right_logical(tile, 8) == me).astype(jnp.int32)
        lists[OWN_B + own_n] = b
        lists[OWN_T + own_n] = tile
        lists[OTH_B + oth_n] = b
        lists[OTH_T + oth_n] = tile
        lists[COUNT + b] = count_ref[b]
        return own_n + own, oth_n + 1 - own

    lax.fori_loop(0, BLK, step, (jnp.int32(0), jnp.int32(0)), unroll=4)


def cell_matrix(b, lists, index, weight):
    lanes = lax.broadcasted_iota(jnp.int32, (4, BLOCK), 1)
    points = lax.broadcasted_iota(jnp.int32, (BLOCK, BLOCK), 0).astype(F32).astype(BF16)
    raw = index[b]
    wgt = jnp.where(lanes < lists[COUNT + b], weight[b], 0.0)
    sums = []
    for k in range(4):
        total = wgt[k : k + 1]
        for j in range(k + 1, 4):
            same = raw[j : j + 1] == raw[k : k + 1]
            total = total + jnp.where(same, wgt[j : j + 1], 0.0)
        sums.append(total.astype(BF16))
    idx = raw.astype(F32).astype(BF16)
    mat = jnp.where(points == idx[3:4], sums[3], jnp.bfloat16(0))
    for k in (2, 1, 0):
        mat = jnp.where(points == idx[k : k + 1], sums[k], mat)
    return mat


def spread_block(heights, mat):
    hi = heights.astype(BF16)
    lo = (heights - hi.astype(F32)).astype(BF16)
    both = lax.dot_general(
        jnp.concatenate([hi, lo], axis=0),
        mat,
        (((1,), (1,)), ((), ())),
        preferred_element_type=F32,
    )
    return both[:NF] + both[NF:]


def other_kernel(
    tile_hbm, count_hbm, ssh_hbm, index_hbm, weight_hbm, lists, wt_out, out,
    tile_ref, count_ref, ssh, index, weight, sems
):
    step = pl.program_id(0)

    @pl.when(step == 0)
    def _():
        pairs = [
            (tile_hbm, tile_ref),
            (count_hbm, count_ref),
            (index_hbm, index),
            (weight_hbm, weight),
            (ssh_hbm, ssh),
        ]
        copies = [pltpu.make_async_copy(s, d, sems.at[i]) for i, (s, d) in enumerate(pairs)]
        for copy in copies:
            copy.start()
        copies[0].wait()
        copies[1].wait()
        make_lists(tile_ref, count_ref, lists)
        me = lax.axis_index(AXES)
        lane = lax.broadcasted_iota(jnp.int32, (NF, BLOCK), 1)
        row = lax.broadcasted_iota(jnp.int32, (NF, BLOCK), 0)
        codes = jnp.zeros((NF, BLOCK), jnp.int32)
        for i in range(HALF_BLK):
            tile = lists[OTH_T + i]
            code = jnp.where(row == 0, tile & 255, lax.shift_right_logical(tile, 8) - me)
            codes = jnp.where((lane == i) & (row < 2), code, codes)
        out[HALF_BLK] = codes.astype(F32).astype(BF16)
        for copy in copies[2:]:
            copy.wait()

    for i in range(STEP):
        b = lists[OTH_B + step * STEP + i]
        mat = cell_matrix(b, lists, index, weight)
        wt_out[i] = mat
        out[step * STEP + i] = spread_block(ssh[b], mat).astype(BF16)


def spread_other(block_tile, cell_count, ssh, index, weight):
    return pl.pallas_call(
        other_kernel,
        grid=(HALF_BLK // STEP,),
        out_shape=(
            jax.ShapeDtypeStruct((LISTS,), jnp.int32),
            jax.ShapeDtypeStruct((HALF_BLK, BLOCK, BLOCK), BF16),
            jax.ShapeDtypeStruct((HALF_BLK + 1, NF, BLOCK), BF16),
        ),
        in_specs=[pl.BlockSpec(memory_space=pltpu.HBM)] * 5,
        out_specs=(
            smem_spec(),
            pl.BlockSpec((STEP, BLOCK, BLOCK), lambda i: (i, 0, 0)),
            vmem_spec(),
        ),
        scratch_shapes=[
            SMEM((BLK,), jnp.int32),
            SMEM((BLK,), jnp.int32),
            VMEM((BLK, NF, BLOCK), F32),
            VMEM((BLK, 4, BLOCK), jnp.int32),
            VMEM((BLK, 4, BLOCK), F32),
            pltpu.SemaphoreType.DMA((5,)),
        ],
        compiler_params=params(63),
        cost_estimate=cost(5),
    )(block_tile, cell_count, ssh, index, weight)


def own_kernel(lists, ssh, index, weight, wt_out, grid):
    flip = jnp.where(lax.axis_index(AXES) >= DEVS // 2, 0xF0, 0)
    grid[...] = jnp.zeros_like(grid)

    def step(j, carry):
        for i in range(STEP):
            slot = j * STEP + i
            b = lists[OWN_B + slot]
            mat = cell_matrix(b, lists, index, weight)
            wt_out[slot] = mat
            tile = (lists[OWN_T + slot] & 255) ^ flip
            grid[tile] = grid[tile] + spread_block(ssh[b], mat)
        return carry

    lax.fori_loop(0, HALF_BLK // STEP, step, 0)


def spread_own(lists, ssh, index, weight):
    return pl.pallas_call(
        own_kernel,
        out_shape=(
            jax.ShapeDtypeStruct((HALF_BLK, BLOCK, BLOCK), BF16),
            jax.ShapeDtypeStruct((TILES + 1, NF, BLOCK), F32),
        ),
        in_specs=[smem_spec()] + [plain_spec()] * 3,
        out_specs=(vmem_spec(),) * 2,
        compiler_params=params(8),
        cost_estimate=cost(5),
    )(lists, ssh, index, weight)


def forward_kernel(
    start_grid, near, far, second, twc, tws, out, spots, grid, mid, wide, codes, sem
):
    del start_grid
    me = lax.axis_index(AXES)
    flip = jnp.where(me >= DEVS // 2, 0xF0, 0)
    rows = []
    from_below = jnp.where((me & 1) == 0, 1, -1)
    for values, direction in ((far, from_below), (near, -from_below)):
        code = values[HALF_BLK].astype(F32).astype(jnp.int32)
        rows.append(jnp.where(code[1:2] == direction, code[0:1] ^ flip, TILES))
    codes[0:2] = jnp.concatenate(rows, axis=0)[:, 0:128]
    copy = pltpu.make_async_copy(codes, spots, sem)
    copy.start()
    copy.wait()

    def add_other(i, carry):
        for side, values in enumerate((far, near)):
            spot = spots[side, i]
            grid[spot] = grid[spot] + values[i].astype(F32)
        return carry

    lax.fori_loop(0, HALF_BLK, add_other, 0, unroll=4)

    def circle(r):
        for h in range(2):
            lanes = slice(h * 128, h * 128 + 128)
            re, im = real_dft16([grid[r * RADIX + s, :, lanes] for s in range(RADIX)])
            for u in range(RADIX):
                v = min(u, RADIX - u)
                cu, su = twc[u : u + 1, lanes], tws[u : u + 1, lanes]
                if u == 0:
                    x, y = re[0], jnp.zeros_like(re[0])
                elif u == 8:
                    x, y = re[8] * cu, -(re[8] * su)
                elif u < 8:
                    x, y = re[v] * cu + im[v] * su, im[v] * cu - re[v] * su
                else:
                    x, y = re[v] * cu - im[v] * su, -(im[v] * cu + re[v] * su)
                rows = slice(u * NF, u * NF + NF)
                mid[r, rows, h * 128 : h * 128 + 128] = x.astype(BF16)
                mid[r, rows, 256 + h * 128 : 256 + h * 128 + 128] = y.astype(BF16)

    def waves(r):
        res = lax.dot_general(
            second[...], mid[r], (((1,), (1,)), ((), ())), preferred_element_type=F32
        )
        res = (res[:128] + res[128:]) * (1.0 / 4096.0)
        for c in range(2):
            for uh in range(2):
                wide[pl.ds(uh * 32 + c * 16 + r, NQ, stride=64), :] = res[
                    c * NQ : c * NQ + NQ, uh * 128 : uh * 128 + 128
                ]

    circle(0)
    for r in range(1, LAT):
        waves(r - 1)
        circle(r)
    waves(LAT - 1)
    out[...] = wide[...].astype(BF16).reshape(out.shape)


def forward(grid, far, near, tables):
    fourier, spots, _ = pl.pallas_call(
        forward_kernel,
        out_shape=(
            jax.ShapeDtypeStruct((DEVS, 32, 128), BF16),
            jax.ShapeDtypeStruct((8, 128), jnp.int32),
            jax.ShapeDtypeStruct((TILES + 1, NF, BLOCK), F32),
        ),
        in_specs=[vmem_spec()] * 3 + [plain_spec()] * 3,
        out_specs=(vmem_spec(), smem_spec(), vmem_spec()),
        scratch_shapes=[
            VMEM((LAT, RADIX * NF, 2 * BLOCK), BF16),
            VMEM((DEVS * 32, 128), F32),
            VMEM((8, 128), jnp.int32),
            pltpu.SemaphoreType.DMA,
        ],
        input_output_aliases={0: 2},
        compiler_params=params(14),
        cost_estimate=cost(8),
    )(grid, near, far, tables["second"], tables["twc"], tables["tws"])
    return fourier, spots


def legendre_kernel(table, data, gauss, love, out, ins, coefs):
    first_order = lax.axis_index(AXES) * ORD
    gw = gauss[...]
    for c in range(2):
        north = jnp.concatenate([data[i, c * 16 : c * 16 + 16] for i in range(64)], axis=0)
        south = jnp.concatenate([data[127 - i, c * 16 : c * 16 + 16] for i in range(64)], axis=0)
        north = north.astype(F32).T
        south = south.astype(F32).T
        even = ((north + south) * gw).astype(BF16)
        odd = ((north - south) * gw).astype(BF16)
        ins[:, c * 16 : c * 16 + 16, :] = even.reshape(ORD, NF, NLAT)
        ins[:, 32 + c * 16 : 32 + c * 16 + 16, :] = odd.reshape(ORD, NF, NLAT)
    degree = lax.broadcasted_iota(jnp.int32, (32, NDEG), 1)
    lane_order = lax.shift_right_logical(lax.broadcasted_iota(jnp.int32, (NLAT, 256), 1), 4) & 3
    for high in range(2):
        for low in range(4):
            k = high * 4 + low
            both = jnp.dot(ins[k], table[k], preferred_element_type=F32)
            order = first_order + k
            is_even = ((degree + order) & 1) == 0
            coef = jnp.where(is_even, both[:32], both[32:])
            coef = jnp.where(degree < order, 0.0, coef)
            coef = coef * love[...]
            mirror = jnp.where(is_even, coef, -coef)
            for side, values in enumerate((coef, mirror)):
                for c in range(2):
                    spot = side * 128 + c * 64 + low * NF
                    coefs[high, spot : spot + NF, :] = values[c * NF : c * NF + NF].astype(BF16)
        columns = coefs[high].T
        total = jnp.zeros((NLAT, 256), F32)
        for low in range(4):
            res = jnp.dot(table[high * 4 + low], columns, preferred_element_type=F32)
            total = jnp.where(lane_order == low, res, total)
        total = total.astype(BF16)
        for i in range(64):
            rows = slice(i * 16, i * 16 + 16)
            out[i, high * 16 : high * 16 + 16] = total[rows, 0:128]
            out[127 - i, high * 16 : high * 16 + 16] = total[rows, 128:256]


def legendre_both(table, data, gauss, love):
    return pl.pallas_call(
        legendre_kernel,
        out_shape=jax.ShapeDtypeStruct((DEVS, 32, 128), BF16),
        in_specs=[plain_spec(), vmem_spec(), plain_spec(), plain_spec()],
        out_specs=vmem_spec(),
        scratch_shapes=[VMEM((ORD, 64, NLAT), BF16), VMEM((2, 256, NDEG), BF16)],
        compiler_params=params(12),
        cost_estimate=cost(11),
    )(table, data, gauss.reshape(1, NLAT), love.reshape(1, NDEG))


def inverse_kernel(
    lists, spots, data, second, twc, tws, own, far, near, wide, tiles, waves
):
    me = lax.axis_index(AXES)
    flip = jnp.where(me >= DEVS // 2, 0xF0, 0)
    wide[...] = data[...].astype(F32).reshape(wide.shape)
    row = lax.broadcasted_iota(jnp.int32, (NQ, 128), 0)
    lane = lax.broadcasted_iota(jnp.int32, (NQ, 128), 1)
    zonal = jnp.where((row == 0) & ((lane & 63) < NF), 1.0, 2.0)
    left = lane < 64

    def spread_waves(r):
        parts = [[], []]
        for uh in range(2):
            first = wide[pl.ds(uh * 32 + r, NQ, stride=64), :] * (2.0 if uh else zonal)
            second_half = wide[pl.ds(uh * 32 + 16 + r, NQ, stride=64), :] * 2.0
            turned = pltpu.roll(jnp.where(left, second_half, first), 64, 1)
            parts[0].append(jnp.where(left, first, turned))
            parts[1].append(jnp.where(left, turned, second_half))
        parts = [jnp.concatenate(part, axis=1) for part in parts]
        spectrum = jnp.concatenate(parts, axis=0).T.astype(BF16)
        spectrum = jnp.concatenate([spectrum, spectrum], axis=1)
        waves[r] = jnp.dot(spectrum, second[...], preferred_element_type=F32)

    def circle(r):
        for h in range(2):
            lanes = slice(h * 128, h * 128 + 128)
            re, im = {}, {}
            for u in range(RADIX):
                rows = slice(u * NF, u * NF + NF)
                x = waves[r, rows, h * 128 : h * 128 + 128]
                y = waves[r, rows, 256 + h * 128 : 256 + h * 128 + 128]
                cu, su = twc[u : u + 1, lanes], tws[u : u + 1, lanes]
                re[u] = x * cu - y * su if u else x
                if u not in (0, 8):
                    im[u] = x * su + y * cu
            a = [re[0]] + [re[u] + re[RADIX - u] for u in range(1, 8)] + [re[8]]
            b = [None] + [im[u] - im[RADIX - u] for u in range(1, 8)]
            values = real_idft16(a, b)
            for s in range(RADIX):
                tiles[r * RADIX + s, :, lanes] = values[s]

    spread_waves(0)
    for r in range(1, LAT):
        spread_waves(r)
        circle(r - 1)
    circle(LAT - 1)

    def gather(i, carry):
        own[i] = tiles[(lists[OWN_T + i] & 255) ^ flip]
        far[i] = tiles[spots[0, i] & 255].astype(BF16)
        near[i] = tiles[spots[1, i] & 255].astype(BF16)
        return carry

    lax.fori_loop(0, HALF_BLK, gather, 0, unroll=4)


def inverse(lists, spots, data, tables):
    return pl.pallas_call(
        inverse_kernel,
        out_shape=(
            jax.ShapeDtypeStruct((HALF_BLK, NF, BLOCK), F32),
            jax.ShapeDtypeStruct((HALF_BLK, NF, BLOCK), BF16),
            jax.ShapeDtypeStruct((HALF_BLK, NF, BLOCK), BF16),
        ),
        in_specs=[smem_spec()] * 2 + [vmem_spec()] + [plain_spec()] * 3,
        out_specs=(vmem_spec(),) * 3,
        scratch_shapes=[
            VMEM((DEVS * 32, 128), F32),
            VMEM((TILES, NF, BLOCK), F32),
            VMEM((LAT, RADIX * NF, 2 * BLOCK), F32),
        ],
        compiler_params=params(20),
        cost_estimate=cost(7),
    )(lists, spots, data, tables["second"], tables["twc"], tables["tws"])


def own_cells_kernel(lists, values, wt, out, res, sems):
    copies = []
    for i in range(HALF_BLK):
        val = values[i]
        hi = val.astype(BF16)
        lo = (val - hi.astype(F32)).astype(BF16)
        both = jnp.dot(jnp.concatenate([hi, lo], axis=0), wt[i], preferred_element_type=F32)
        res[i] = both[:NF] + both[NF:]
        copy = pltpu.make_async_copy(res.at[i], out.at[lists[OWN_B + i]], sems.at[i])
        copy.start()
        copies.append(copy)
    for copy in copies:
        copy.wait()


def own_cells(lists, values, wt):
    return pl.pallas_call(
        own_cells_kernel,
        out_shape=jax.ShapeDtypeStruct((BLK, NF, BLOCK), F32),
        in_specs=[smem_spec()] + [vmem_spec()] * 2,
        out_specs=pl.BlockSpec(memory_space=pltpu.HBM),
        scratch_shapes=[VMEM((HALF_BLK, NF, BLOCK), F32), pltpu.SemaphoreType.DMA((HALF_BLK,))],
        compiler_params=params(6),
        cost_estimate=cost(2),
    )(lists, values, wt)


def cells_kernel(lists, own, far, near, wt, out, res, sems):
    del own
    me = lax.axis_index(AXES)
    odd = (me & 1) == 1
    copies = []
    for i in range(HALF_BLK):
        above = lax.shift_right_logical(lists[OTH_T + i], 8) > me
        val = jnp.where(above == odd, far[i], near[i])
        res[i] = jnp.dot(val, wt[i], preferred_element_type=F32)
        copy = pltpu.make_async_copy(res.at[i], out.at[lists[OTH_B + i]], sems.at[i])
        copy.start()
        copies.append(copy)
    for copy in copies:
        copy.wait()


def all_cells(lists, own, far, near, wt):
    return pl.pallas_call(
        cells_kernel,
        out_shape=jax.ShapeDtypeStruct((BLK, NF, BLOCK), F32),
        in_specs=[smem_spec(), pl.BlockSpec(memory_space=pltpu.HBM)]
        + [vmem_spec()] * 2
        + [plain_spec()],
        out_specs=pl.BlockSpec(memory_space=pltpu.HBM),
        scratch_shapes=[VMEM((HALF_BLK, NF, BLOCK), F32), pltpu.SemaphoreType.DMA((HALF_BLK,))],
        input_output_aliases={1: 0},
        compiler_params=params(8),
        cost_estimate=cost(4),
    )(lists, own, far, near, wt)


def swap(value, first):
    pairs = []
    for i in range(first, DEVS - 1, 2):
        pairs += [(i, i + 1), (i + 1, i)]
    return lax.ppermute(value, AXES, pairs)


def on_device(
    tables, ssh, cell_count, remap_index, remap_weight, block_tile, gauss_weight, love, legendre
):
    lists, wt_oth, oth = spread_other(block_tile, cell_count, ssh, remap_index, remap_weight)
    far = swap(oth, 1)
    near = swap(oth, 0)
    wt_own, grid = spread_own(lists, ssh, remap_index, remap_weight)
    fourier, spots = forward(grid, far, near, tables)
    by_order = lax.all_to_all(fourier, AXES, split_axis=0, concat_axis=0, tiled=True)
    synth = legendre_both(legendre, by_order, gauss_weight, love)
    by_lat = lax.all_to_all(synth, AXES, split_axis=0, concat_axis=0, tiled=True)
    own_v, far_v, near_v = inverse(lists, spots, by_lat, tables)
    from_far = swap(far_v, 1)
    from_near = swap(near_v, 0)
    own_cell = own_cells(lists, own_v, wt_own)
    return all_cells(lists, own_cell, from_far, from_near, wt_oth)


def solution(mesh):
    tables = {name: jnp.asarray(table) for name, table in make_tables().items()}
    return jax.shard_map(
        functools.partial(on_device, tables),
        mesh=mesh,
        in_specs=(
            P(AXES, None, None),
            P(AXES),
            P(AXES, None, None),
            P(AXES, None, None),
            P(AXES),
            P(),
            P(),
            P(AXES, None, None),
        ),
        out_specs=P(AXES, None, None),
        check_vma=False,
    )
```

```python
import functools
import math

import jax
import jax.numpy as jnp
import numpy as np
from jax import lax
from jax.experimental import pallas as pl
from jax.experimental.pallas import tpu as pltpu
from jax.sharding import PartitionSpec as P

AXES = ("dom", "order")
DEVS = 128
NF = 16
BLOCK = 256
BLK = 64
HALF_BLK = 32
TILES = 256
LAT = 16
ORD = 8
NLAT = 1024
NDEG = 1024
RADIX = 16
NQ = 64
STEP = 8
F32 = jnp.float32
BF16 = jnp.bfloat16
MIB = 1 << 20

SMEM = pltpu.SMEM
VMEM = pltpu.VMEM


def hi_lo(table):
    table = np.asarray(table, np.float32)
    hi = table.astype(jnp.bfloat16)
    lo = (table - hi.astype(np.float32)).astype(jnp.bfloat16)
    return hi, lo


def make_tables():
    points = np.arange(BLOCK)
    angle = 2 * np.pi * ((np.arange(NQ)[:, None] * points[None, :]) % BLOCK) / BLOCK
    cos, sin = np.cos(angle), np.sin(angle)
    second = np.concatenate(
        [np.concatenate([cos, sin], axis=1), np.concatenate([-sin, cos], axis=1)], axis=0
    )
    s_hi, s_lo = hi_lo(2.0 * second)
    twist = 2 * np.pi * (np.arange(RADIX)[:, None] * points[None, :]) / 4096.0
    return dict(
        second=np.concatenate([s_hi, s_lo], axis=0),
        twc=np.cos(twist).astype(np.float32),
        tws=np.sin(twist).astype(np.float32),
    )


ROOT = math.sqrt(0.5)
COS1 = math.cos(math.pi / 8)
SIN1 = math.sin(math.pi / 8)


def real_dft16(g):
    e = [g[s] + g[s + 8] for s in range(8)]
    o = [g[s] - g[s + 8] for s in range(8)]
    re, im = [None] * 9, [None] * 9
    ee = [e[s] + e[s + 4] for s in range(4)]
    eo = [e[s] - e[s + 4] for s in range(4)]
    x, y = ee[0] + ee[2], ee[1] + ee[3]
    re[0], re[8] = x + y, x - y
    re[4], im[4] = ee[0] - ee[2], ee[3] - ee[1]

    def odd4(p):
        d, s = (p[1] - p[3]) * ROOT, (p[1] + p[3]) * ROOT
        return (p[0] + d, -(s + p[2])), (p[0] - d, p[2] - s)

    (re[2], im[2]), (re[6], im[6]) = odd4(eo)
    a1, a3 = odd4(o[0::2])
    b1, b3 = odd4(o[1::2])
    t = (b1[0] * COS1 + b1[1] * SIN1, b1[1] * COS1 - b1[0] * SIN1)
    re[1], im[1] = a1[0] + t[0], a1[1] + t[1]
    re[7], im[7] = a1[0] - t[0], t[1] - a1[1]
    t = (b3[0] * SIN1 + b3[1] * COS1, b3[1] * SIN1 - b3[0] * COS1)
    re[3], im[3] = a3[0] + t[0], a3[1] + t[1]
    re[5], im[5] = a3[0] - t[0], t[1] - a3[1]
    return re, im


def real_idft16(a, b):
    x, z = a[0] + a[8], a[0] - a[8]
    q = [x + a[4], z - b[4], x - a[4], z + b[4]]

    def odd4(p1, p3):
        d, s = (p1[0] - p3[0]) * ROOT, (p1[1] + p3[1]) * ROOT
        return [p1[0] + p3[0], d - s, p3[1] - p1[1], -(d + s)]

    w = odd4((a[2], b[2]), (a[6], b[6]))
    even = [q[t] + w[t] for t in range(4)] + [q[t] - w[t] for t in range(4)]
    p1, q1 = (a[1] + a[7], b[1] - b[7]), (a[1] - a[7], b[1] + b[7])
    p3, q3 = (a[3] + a[5], b[3] - b[5]), (a[3] - a[5], b[3] + b[5])
    q1 = (q1[0] * COS1 - q1[1] * SIN1, q1[0] * SIN1 + q1[1] * COS1)
    q3 = (q3[0] * SIN1 - q3[1] * COS1, q3[0] * COS1 + q3[1] * SIN1)
    oe, oo = odd4(p1, p3), odd4(q1, q3)
    odd = [oe[s // 2] if s % 2 == 0 else oo[s // 2] for s in range(8)]
    return [even[s] + odd[s] for s in range(8)] + [even[s] - odd[s] for s in range(8)]


def vmem_spec():
    return pl.BlockSpec(memory_space=VMEM)


def smem_spec():
    return pl.BlockSpec(memory_space=SMEM)


def plain_spec():
    return pl.BlockSpec()


def cost(micros):
    return pl.CostEstimate(flops=micros * 10**9, bytes_accessed=4 * MIB, transcendentals=0)


def params(mib):
    return pltpu.CompilerParams(vmem_limit_bytes=mib * MIB)


OWN_B, OWN_T, OTH_B, OTH_T, COUNT, LISTS = 0, 40, 80, 120, 160, 224


def make_lists(tile_ref, count_ref, lists):
    me = lax.axis_index(AXES)

    def step(b, counts):
        own_n, oth_n = counts
        tile = tile_ref[b]
        own = (lax.shift_right_logical(tile, 8) == me).astype(jnp.int32)
        lists[OWN_B + own_n] = b
        lists[OWN_T + own_n] = tile
        lists[OTH_B + oth_n] = b
        lists[OTH_T + oth_n] = tile
        lists[COUNT + b] = count_ref[b]
        return own_n + own, oth_n + 1 - own

    lax.fori_loop(0, BLK, step, (jnp.int32(0), jnp.int32(0)), unroll=4)


def cell_matrix(b, lists, index, weight):
    lanes = lax.broadcasted_iota(jnp.int32, (4, BLOCK), 1)
    points = lax.broadcasted_iota(jnp.int32, (BLOCK, BLOCK), 0).astype(F32).astype(BF16)
    raw = index[b]
    wgt = jnp.where(lanes < lists[COUNT + b], weight[b], 0.0)
    sums = []
    for k in range(4):
        total = wgt[k : k + 1]
        for j in range(k + 1, 4):
            same = raw[j : j + 1] == raw[k : k + 1]
            total = total + jnp.where(same, wgt[j : j + 1], 0.0)
        sums.append(total.astype(BF16))
    idx = raw.astype(F32).astype(BF16)
    mat = jnp.where(points == idx[3:4], sums[3], jnp.bfloat16(0))
    for k in (2, 1, 0):
        mat = jnp.where(points == idx[k : k + 1], sums[k], mat)
    return mat


def spread_block(heights, mat):
    hi = heights.astype(BF16)
    lo = (heights - hi.astype(F32)).astype(BF16)
    both = lax.dot_general(
        jnp.concatenate([hi, lo], axis=0),
        mat,
        (((1,), (1,)), ((), ())),
        preferred_element_type=F32,
    )
    return both[:NF] + both[NF:]


def other_kernel(
    tile_hbm, count_hbm, ssh_hbm, index_hbm, weight_hbm, lists, wt_out, out,
    tile_ref, count_ref, ssh, index, weight, sems
):
    step = pl.program_id(0)

    @pl.when(step == 0)
    def _():
        pairs = [
            (tile_hbm, tile_ref),
            (count_hbm, count_ref),
            (index_hbm, index),
            (weight_hbm, weight),
            (ssh_hbm, ssh),
        ]
        copies = [pltpu.make_async_copy(s, d, sems.at[i]) for i, (s, d) in enumerate(pairs)]
        for copy in copies:
            copy.start()
        copies[0].wait()
        copies[1].wait()
        make_lists(tile_ref, count_ref, lists)
        me = lax.axis_index(AXES)
        lane = lax.broadcasted_iota(jnp.int32, (NF, BLOCK), 1)
        row = lax.broadcasted_iota(jnp.int32, (NF, BLOCK), 0)
        codes = jnp.zeros((NF, BLOCK), jnp.int32)
        for i in range(HALF_BLK):
            tile = lists[OTH_T + i]
            code = jnp.where(row == 0, tile & 255, lax.shift_right_logical(tile, 8) - me)
            codes = jnp.where((lane == i) & (row < 2), code, codes)
        out[HALF_BLK] = codes.astype(F32).astype(BF16)
        for copy in copies[2:]:
            copy.wait()

    for i in range(STEP):
        b = lists[OTH_B + step * STEP + i]
        mat = cell_matrix(b, lists, index, weight)
        wt_out[i] = mat
        out[step * STEP + i] = spread_block(ssh[b], mat).astype(BF16)


def spread_other(block_tile, cell_count, ssh, index, weight):
    return pl.pallas_call(
        other_kernel,
        grid=(HALF_BLK // STEP,),
        out_shape=(
            jax.ShapeDtypeStruct((LISTS,), jnp.int32),
            jax.ShapeDtypeStruct((HALF_BLK, BLOCK, BLOCK), BF16),
            jax.ShapeDtypeStruct((HALF_BLK + 1, NF, BLOCK), BF16),
        ),
        in_specs=[pl.BlockSpec(memory_space=pltpu.HBM)] * 5,
        out_specs=(
            smem_spec(),
            pl.BlockSpec((STEP, BLOCK, BLOCK), lambda i: (i, 0, 0)),
            vmem_spec(),
        ),
        scratch_shapes=[
            SMEM((BLK,), jnp.int32),
            SMEM((BLK,), jnp.int32),
            VMEM((BLK, NF, BLOCK), F32),
            VMEM((BLK, 4, BLOCK), jnp.int32),
            VMEM((BLK, 4, BLOCK), F32),
            pltpu.SemaphoreType.DMA((5,)),
        ],
        compiler_params=params(63),
        cost_estimate=cost(5),
    )(block_tile, cell_count, ssh, index, weight)


def own_kernel(lists, ssh, index, weight, wt_out, grid):
    flip = jnp.where(lax.axis_index(AXES) >= DEVS // 2, 0xF0, 0)
    grid[...] = jnp.zeros_like(grid)

    def step(j, carry):
        for i in range(STEP):
            slot = j * STEP + i
            b = lists[OWN_B + slot]
            mat = cell_matrix(b, lists, index, weight)
            wt_out[slot] = mat
            tile = (lists[OWN_T + slot] & 255) ^ flip
            grid[tile] = grid[tile] + spread_block(ssh[b], mat)
        return carry

    lax.fori_loop(0, HALF_BLK // STEP, step, 0)


def spread_own(lists, ssh, index, weight):
    return pl.pallas_call(
        own_kernel,
        out_shape=(
            jax.ShapeDtypeStruct((HALF_BLK, BLOCK, BLOCK), BF16),
            jax.ShapeDtypeStruct((TILES + 1, NF, BLOCK), F32),
        ),
        in_specs=[smem_spec()] + [plain_spec()] * 3,
        out_specs=(vmem_spec(),) * 2,
        compiler_params=params(8),
        cost_estimate=cost(5),
    )(lists, ssh, index, weight)


def forward_kernel(
    start_grid, near, far, second, twc, tws, out, spots, grid, mid, wide, codes, sem
):
    del start_grid
    me = lax.axis_index(AXES)
    flip = jnp.where(me >= DEVS // 2, 0xF0, 0)
    rows = []
    from_below = jnp.where((me & 1) == 0, 1, -1)
    for values, direction in ((far, from_below), (near, -from_below)):
        code = values[HALF_BLK].astype(F32).astype(jnp.int32)
        rows.append(jnp.where(code[1:2] == direction, code[0:1] ^ flip, TILES))
    codes[0:2] = jnp.concatenate(rows, axis=0)[:, 0:128]
    copy = pltpu.make_async_copy(codes, spots, sem)
    copy.start()
    copy.wait()

    def add_other(i, carry):
        for side, values in enumerate((far, near)):
            spot = spots[side, i]
            grid[spot] = grid[spot] + values[i].astype(F32)
        return carry

    lax.fori_loop(0, HALF_BLK, add_other, 0, unroll=4)

    def circle(r):
        for h in range(2):
            lanes = slice(h * 128, h * 128 + 128)
            re, im = real_dft16([grid[r * RADIX + s, :, lanes] for s in range(RADIX)])
            for u in range(RADIX):
                v = min(u, RADIX - u)
                cu, su = twc[u : u + 1, lanes], tws[u : u + 1, lanes]
                if u == 0:
                    x, y = re[0], jnp.zeros_like(re[0])
                elif u == 8:
                    x, y = re[8] * cu, -(re[8] * su)
                elif u < 8:
                    x, y = re[v] * cu + im[v] * su, im[v] * cu - re[v] * su
                else:
                    x, y = re[v] * cu - im[v] * su, -(im[v] * cu + re[v] * su)
                rows = slice(u * NF, u * NF + NF)
                mid[r, rows, h * 128 : h * 128 + 128] = x.astype(BF16)
                mid[r, rows, 256 + h * 128 : 256 + h * 128 + 128] = y.astype(BF16)

    def waves(r):
        res = lax.dot_general(
            second[...], mid[r], (((1,), (1,)), ((), ())), preferred_element_type=F32
        )
        res = (res[:128] + res[128:]) * (1.0 / 8192.0)
        for c in range(2):
            for uh in range(2):
                wide[pl.ds(uh * 32 + c * 16 + r, NQ, stride=64), :] = res[
                    c * NQ : c * NQ + NQ, uh * 128 : uh * 128 + 128
                ]

    circle(0)
    for r in range(1, LAT):
        waves(r - 1)
        circle(r)
    waves(LAT - 1)
    out[...] = wide[...].astype(BF16).reshape(out.shape)


def forward(grid, far, near, tables):
    fourier, spots, _ = pl.pallas_call(
        forward_kernel,
        out_shape=(
            jax.ShapeDtypeStruct((DEVS, 32, 128), BF16),
            jax.ShapeDtypeStruct((8, 128), jnp.int32),
            jax.ShapeDtypeStruct((TILES + 1, NF, BLOCK), F32),
        ),
        in_specs=[vmem_spec()] * 3 + [plain_spec()] * 3,
        out_specs=(vmem_spec(), smem_spec(), vmem_spec()),
        scratch_shapes=[
            VMEM((LAT, RADIX * NF, 2 * BLOCK), BF16),
            VMEM((DEVS * 32, 128), F32),
            VMEM((8, 128), jnp.int32),
            pltpu.SemaphoreType.DMA,
        ],
        input_output_aliases={0: 2},
        compiler_params=params(14),
        cost_estimate=cost(8),
    )(grid, near, far, tables["second"], tables["twc"], tables["tws"])
    return fourier, spots


def legendre_kernel(table, data, gauss, love, out, ins, coefs):
    first_order = lax.axis_index(AXES) * ORD
    gw = gauss[...]
    for c in range(2):
        north = jnp.concatenate([data[i, c * 16 : c * 16 + 16] for i in range(64)], axis=0)
        south = jnp.concatenate([data[127 - i, c * 16 : c * 16 + 16] for i in range(64)], axis=0)
        north = north.astype(F32).T
        south = south.astype(F32).T
        even = ((north + south) * gw).astype(BF16)
        odd = ((north - south) * gw).astype(BF16)
        ins[:, c * 16 : c * 16 + 16, :] = even.reshape(ORD, NF, NLAT)
        ins[:, 32 + c * 16 : 32 + c * 16 + 16, :] = odd.reshape(ORD, NF, NLAT)
    degree = lax.broadcasted_iota(jnp.int32, (32, NDEG), 1)
    lane_order = lax.shift_right_logical(lax.broadcasted_iota(jnp.int32, (NLAT, 256), 1), 4) & 3
    for high in range(2):
        for low in range(4):
            k = high * 4 + low
            both = jnp.dot(ins[k], table[k], preferred_element_type=F32)
            order = first_order + k
            is_even = ((degree + order) & 1) == 0
            coef = jnp.where(is_even, both[:32], both[32:])
            coef = jnp.where(degree < order, 0.0, coef)
            coef = coef * love[...]
            mirror = jnp.where(is_even, coef, -coef)
            for side, values in enumerate((coef, mirror)):
                for c in range(2):
                    spot = side * 128 + c * 64 + low * NF
                    coefs[high, spot : spot + NF, :] = values[c * NF : c * NF + NF].astype(BF16)
        columns = coefs[high].T
        total = jnp.zeros((NLAT, 256), F32)
        for low in range(4):
            res = jnp.dot(table[high * 4 + low], columns, preferred_element_type=F32)
            total = jnp.where(lane_order == low, res, total)
        total = total.astype(BF16)
        for i in range(64):
            rows = slice(i * 16, i * 16 + 16)
            out[i, high * 16 : high * 16 + 16] = total[rows, 0:128]
            out[127 - i, high * 16 : high * 16 + 16] = total[rows, 128:256]


def legendre_both(table, data, gauss, love):
    return pl.pallas_call(
        legendre_kernel,
        out_shape=jax.ShapeDtypeStruct((DEVS, 32, 128), BF16),
        in_specs=[plain_spec(), vmem_spec(), plain_spec(), plain_spec()],
        out_specs=vmem_spec(),
        scratch_shapes=[VMEM((ORD, 64, NLAT), BF16), VMEM((2, 256, NDEG), BF16)],
        compiler_params=params(12),
        cost_estimate=cost(11),
    )(table, data, gauss.reshape(1, NLAT), love.reshape(1, NDEG))


def inverse_kernel(
    lists, spots, data, second, twc, tws, own, far, near, wide, tiles, waves
):
    me = lax.axis_index(AXES)
    flip = jnp.where(me >= DEVS // 2, 0xF0, 0)
    wide[...] = data[...].astype(F32).reshape(wide.shape)
    row = lax.broadcasted_iota(jnp.int32, (NQ, 128), 0)
    lane = lax.broadcasted_iota(jnp.int32, (NQ, 128), 1)
    zonal = jnp.where((row == 0) & ((lane & 63) < NF), 0.5, 1.0)
    left = lane < 64

    def spread_waves(r):
        parts = [[], []]
        for uh in range(2):
            first = wide[pl.ds(uh * 32 + r, NQ, stride=64), :]
            first = first if uh else first * zonal
            second_half = wide[pl.ds(uh * 32 + 16 + r, NQ, stride=64), :]
            turned = pltpu.roll(jnp.where(left, second_half, first), 64, 1)
            parts[0].append(jnp.where(left, first, turned))
            parts[1].append(jnp.where(left, turned, second_half))
        parts = [jnp.concatenate(part, axis=1) for part in parts]
        spectrum = jnp.concatenate(parts, axis=0).T.astype(BF16)
        spectrum = jnp.concatenate([spectrum, spectrum], axis=1)
        waves[r] = jnp.dot(spectrum, second[...], preferred_element_type=F32)

    def circle(r):
        for h in range(2):
            lanes = slice(h * 128, h * 128 + 128)
            re, im = {}, {}
            for u in range(RADIX):
                rows = slice(u * NF, u * NF + NF)
                x = waves[r, rows, h * 128 : h * 128 + 128]
                y = waves[r, rows, 256 + h * 128 : 256 + h * 128 + 128]
                cu, su = twc[u : u + 1, lanes], tws[u : u + 1, lanes]
                re[u] = x * cu - y * su if u else x
                if u not in (0, 8):
                    im[u] = x * su + y * cu
            a = [re[0]] + [re[u] + re[RADIX - u] for u in range(1, 8)] + [re[8]]
            b = [None] + [im[u] - im[RADIX - u] for u in range(1, 8)]
            values = real_idft16(a, b)
            for s in range(RADIX):
                tiles[r * RADIX + s, :, lanes] = values[s]

    spread_waves(0)
    for r in range(1, LAT):
        spread_waves(r)
        circle(r - 1)
    circle(LAT - 1)

    def gather(i, carry):
        own[i] = tiles[(lists[OWN_T + i] & 255) ^ flip]
        far[i] = tiles[spots[0, i] & 255].astype(BF16)
        near[i] = tiles[spots[1, i] & 255].astype(BF16)
        return carry

    lax.fori_loop(0, HALF_BLK, gather, 0, unroll=4)


def inverse(lists, spots, data, tables):
    return pl.pallas_call(
        inverse_kernel,
        out_shape=(
            jax.ShapeDtypeStruct((HALF_BLK, NF, BLOCK), F32),
            jax.ShapeDtypeStruct((HALF_BLK, NF, BLOCK), BF16),
            jax.ShapeDtypeStruct((HALF_BLK, NF, BLOCK), BF16),
        ),
        in_specs=[smem_spec()] * 2 + [vmem_spec()] + [plain_spec()] * 3,
        out_specs=(vmem_spec(),) * 3,
        scratch_shapes=[
            VMEM((DEVS * 32, 128), F32),
            VMEM((TILES, NF, BLOCK), F32),
            VMEM((LAT, RADIX * NF, 2 * BLOCK), F32),
        ],
        compiler_params=params(20),
        cost_estimate=cost(7),
    )(lists, spots, data, tables["second"], tables["twc"], tables["tws"])


def own_cells_kernel(lists, values, wt, out, res, sems):
    copies = []
    for i in range(HALF_BLK):
        val = values[i]
        hi = val.astype(BF16)
        lo = (val - hi.astype(F32)).astype(BF16)
        both = jnp.dot(jnp.concatenate([hi, lo], axis=0), wt[i], preferred_element_type=F32)
        res[i] = both[:NF] + both[NF:]
        copy = pltpu.make_async_copy(res.at[i], out.at[lists[OWN_B + i]], sems.at[i])
        copy.start()
        copies.append(copy)
    for copy in copies:
        copy.wait()


def own_cells(lists, values, wt):
    return pl.pallas_call(
        own_cells_kernel,
        out_shape=jax.ShapeDtypeStruct((BLK, NF, BLOCK), F32),
        in_specs=[smem_spec()] + [vmem_spec()] * 2,
        out_specs=pl.BlockSpec(memory_space=pltpu.HBM),
        scratch_shapes=[VMEM((HALF_BLK, NF, BLOCK), F32), pltpu.SemaphoreType.DMA((HALF_BLK,))],
        compiler_params=params(6),
        cost_estimate=cost(2),
    )(lists, values, wt)


def cells_kernel(lists, own, far, near, wt, out, res, sems):
    del own
    me = lax.axis_index(AXES)
    odd = (me & 1) == 1
    copies = []
    for i in range(HALF_BLK):
        above = lax.shift_right_logical(lists[OTH_T + i], 8) > me
        val = jnp.where(above == odd, far[i], near[i])
        res[i] = jnp.dot(val, wt[i], preferred_element_type=F32)
        copy = pltpu.make_async_copy(res.at[i], out.at[lists[OTH_B + i]], sems.at[i])
        copy.start()
        copies.append(copy)
    for copy in copies:
        copy.wait()


def all_cells(lists, own, far, near, wt):
    return pl.pallas_call(
        cells_kernel,
        out_shape=jax.ShapeDtypeStruct((BLK, NF, BLOCK), F32),
        in_specs=[smem_spec(), pl.BlockSpec(memory_space=pltpu.HBM)]
        + [vmem_spec()] * 2
        + [plain_spec()],
        out_specs=pl.BlockSpec(memory_space=pltpu.HBM),
        scratch_shapes=[VMEM((HALF_BLK, NF, BLOCK), F32), pltpu.SemaphoreType.DMA((HALF_BLK,))],
        input_output_aliases={1: 0},
        compiler_params=params(8),
        cost_estimate=cost(4),
    )(lists, own, far, near, wt)


def swap(value, first):
    pairs = []
    for i in range(first, DEVS - 1, 2):
        pairs += [(i, i + 1), (i + 1, i)]
    return lax.ppermute(value, AXES, pairs)


def on_device(
    tables, ssh, cell_count, remap_index, remap_weight, block_tile, gauss_weight, love, legendre
):
    lists, wt_oth, oth = spread_other(block_tile, cell_count, ssh, remap_index, remap_weight)
    far = swap(oth, 1)
    near = swap(oth, 0)
    wt_own, grid = spread_own(lists, ssh, remap_index, remap_weight)
    fourier, spots = forward(grid, far, near, tables)
    by_order = lax.all_to_all(fourier, AXES, split_axis=0, concat_axis=0, tiled=True)
    synth = legendre_both(legendre, by_order, gauss_weight, love)
    by_lat = lax.all_to_all(synth, AXES, split_axis=0, concat_axis=0, tiled=True)
    own_v, far_v, near_v = inverse(lists, spots, by_lat, tables)
    from_far = swap(far_v, 1)
    from_near = swap(near_v, 0)
    own_cell = own_cells(lists, own_v, wt_own)
    return all_cells(lists, own_cell, from_far, from_near, wt_oth)


def solution(mesh):
    tables = {name: jnp.asarray(table) for name, table in make_tables().items()}
    return jax.shard_map(
        functools.partial(on_device, tables),
        mesh=mesh,
        in_specs=(
            P(AXES, None, None),
            P(AXES),
            P(AXES, None, None),
            P(AXES, None, None),
            P(AXES),
            P(),
            P(),
            P(AXES, None, None),
        ),
        out_specs=P(AXES, None, None),
        check_vma=False,
    )
```
